256 devices in a mesh: pix: 64 (over z, y, core), lat: 4 (over x).
Axes of the slice: x: 4, y: 4, z: 8, core: 2. Of those that a mesh axis runs over, the one named last changes fastest.
Arguments:
- latents: float32 [2048, 512], P('lat'), as said below
- pixel_keys: float32 [32768, 512], P('pix'), as said below
- pixel_values: float32 [32768, 512], P('pix'), may hold values from -6 to 6
- norm_gain: float32 [512], replicated, may hold values from 0.1 to 1.9
- w_key: float32 [512, 512], replicated, may hold values from -0.25 to 0.25
- w_value: float32 [512, 512], replicated, may hold values from -0.25 to 0.25
- pixel_queries: float32 [32768, 512], P('pix'), as said below
Outputs:
- latent_state: float32 [2048, 512], P('lat')
- pixel_out: float32 [32768, 512], P('pix')
The draws below stay inside these ranges and needn't reach their ends.
Inputs may be any that keep to these rules, and one draw needn't show every extreme that they name: Real-valued latents. `pixel_keys`: Real-valued keys. `pixel_queries`: Real-valued queries.
All inputs are finite; a program needn't handle non-finite values.
Results may differ from the reference program's by a relative error of at most 0.0003.
Values sent between devices are 32-bit elements; how exact they have to be, the bound alone decides.
A program may use at most 64 MiB of HBM per device.

```python
import jax
import jax.numpy as jnp
from jax import lax

D = 512
L = 2048
PIXELS = 32768


def keys_table(key):
    table = 4.0 * jax.random.normal(jax.random.fold_in(key, 11), (PIXELS, D), jnp.float32)
    return table


def draw_pixel_keys(key, part):
    return keys_table(key)


def draw_latents(key, part):
    base = jax.random.normal(jax.random.fold_in(key, 23), (L, D), jnp.float32)
    return base


def draw_pixel_queries(key, part):
    base = jax.random.normal(jax.random.fold_in(key, 31), (PIXELS, D), jnp.float32)
    return base


def level_of(key, shape, cuts, smallest, high):
    level, own = 1.0, jax.random.fold_in(key, 6)
    for position, shards_of in cuts:
        draws = jnp.exp(jax.random.uniform(jax.random.fold_in(own, position), (shards_of,), jnp.float32, smallest / len(cuts), high / len(cuts)))
        level = level * jnp.repeat(draws, shape[position] // shards_of).reshape([-1 if axis == position else 1 for axis in range(len(shape))])
    return level


def scatter_about(rng, dims, scale, bound, split=(), held_as=jnp.bfloat16):
    factor_of = level_of(rng, dims, split, -0.22, 0.18) if split else 1.0
    values = jax.random.normal(rng, dims, jnp.float32) * scale * factor_of
    return jnp.minimum(jnp.maximum(values, -bound), bound).astype(held_as)


def setup_inputs(seed: int = 0) -> dict:
    streams_of = jax.random.split(jax.random.key(seed), 8)
    return {
        "latents": draw_latents(jax.random.fold_in(streams_of[7], 71), 0),
        "pixel_keys": draw_pixel_keys(jax.random.fold_in(streams_of[7], 71), 0),
        "pixel_values": scatter_about(streams_of[2], (PIXELS, D), 1.0, 6.0, ((0, 64),), jnp.float32),
        "norm_gain": jnp.clip(1.0 + 0.18 * jax.random.normal(streams_of[3], (D,), jnp.float32), 0.1, 1.9),
        "w_key": scatter_about(streams_of[4], (D, D), D ** -0.5, 0.25, (), jnp.float32),
        "w_value": scatter_about(streams_of[5], (D, D), D ** -0.5, 0.25, (), jnp.float32),
        "pixel_queries": draw_pixel_queries(jax.random.fold_in(streams_of[7], 71), 0),
    }


def attend(queries, keys, values):
    scores = jnp.dot(queries, keys.T, precision=lax.Precision.HIGHEST) / jnp.sqrt(jnp.float32(D))
    top = lax.optimization_barrier(jnp.max(scores, axis=1, keepdims=True))
    weights = jnp.exp(scores - top)
    total = lax.optimization_barrier(jnp.sum(weights, axis=1, keepdims=True))
    return jnp.dot(weights, values, precision=lax.Precision.HIGHEST) / total

def reference(latents, pixel_keys, pixel_values, norm_gain, w_key, w_value, pixel_queries):
    block = 128
    blocks = latents.reshape(L // block, block, D)
    read = lax.map(lambda rows: attend(rows, pixel_keys, pixel_values), blocks).reshape(L, D)
    latent_state = latents + read
    normed = latent_state / jnp.sqrt(lax.optimization_barrier(jnp.mean(latent_state * latent_state, axis=1, keepdims=True)) + 1e-06) * norm_gain
    latent_keys = jnp.dot(normed, w_key, precision=lax.Precision.HIGHEST)
    latent_values = jnp.dot(normed, w_value, precision=lax.Precision.HIGHEST)
    pblock = min(1024, PIXELS)
    pblocks = pixel_queries.reshape(PIXELS // pblock, pblock, D)
    pixel_out = lax.map(lambda rows: attend(rows, latent_keys, latent_values), pblocks).reshape(PIXELS, D)
    return (latent_state, pixel_out)
```

```python
import functools

import jax
import jax.numpy as jnp
from jax import lax
from jax.experimental import pallas as pl
from jax.experimental.pallas import tpu as pltpu
from jax.sharding import PartitionSpec as P

MESH = pl.DeviceIdType.MESH
F32, BF16 = jnp.float32, jnp.bfloat16
D = 512
NY, NZ, NX = 4, 8, 4
ROWS = 512
HALF = ROWS // 2
GROUP = 8
TILES = D // 128
SLAB = TILES * NZ * GROUP + 16
PIECE = TILES * GROUP + 16
TOP = TILES * NZ * GROUP
NN = (((1,), (0,)), ((), ()))
NT = (((1,), (1,)), ((), ()))
SCALE = 512.0**-0.5


def split(value):
    high = value.astype(BF16)
    return high, (value - high.astype(F32)).astype(BF16)


def dot3(a, b, dims):
    def one(u, v):
        return lax.dot_general(u, v, dims, preferred_element_type=F32)

    return one(a[0], b[0]) + (one(a[0], b[1]) + one(a[1], b[0]))


def kernel(
    lat_in, keys_in, vals_in, gain_in, wk_in, wv_in, q_in, state_out, pix_out,
    lat, keys, vals, gain, wk, wv, q,
    kh, kl, vh, vl, qh, ql, wvh, wvl,
    slab_send, slab_own, slab_sib, slab_c, slab_r, piece, piece_r,
    g, acc, mx, tot, result,
    in_sem, out_sem, a0s, a0r, a1s, a1r, a2s, a2r, g1s, g1r, g2s, g2r, g3s, g3r, cs, cr,
):
    p = lax.axis_index("pix")
    x = lax.axis_index("lat")
    c = lax.rem(p, 2)
    y = lax.rem(p // 2, NY)
    z = p // (2 * NY)

    def at(zz, yy, cc, xx):
        return ((zz * NY + yy) * 2 + cc, xx)

    sib = at(z, y, 1 - c, x)

    def ypeer(d):
        return at(z, lax.rem(y + d + NY, NY), c, x)

    def zpeer(d):
        return at(lax.rem(z + d + NZ, NZ), y, c, x)

    def xpeer(d):
        return at(z, y, c, lax.rem(x + d + NX, NX))

    loads = []
    for k, (src, dst) in enumerate(
        [(lat_in, lat), (keys_in, keys), (vals_in, vals), (q_in, q), (wk_in, wk), (gain_in, gain), (wv_in, wv)]
    ):
        cp = pltpu.make_async_copy(src, dst, in_sem.at[k])
        cp.start()
        loads.append(cp)

    barrier = pltpu.get_barrier_semaphore()
    peers = (
        [sib]
        + [ypeer(d) for d in range(1, NY)]
        + [zpeer(d) for d in range(1, NZ)]
        + [xpeer(d) for d in range(1, NX)]
    )
    for dev in peers:
        pl.semaphore_signal(barrier, inc=1, device_id=dev, device_id_type=MESH)

    def remote(src, dst, ss, rs, dev):
        return pltpu.make_async_remote_copy(
            src_ref=src, dst_ref=dst, send_sem=ss, recv_sem=rs, device_id=dev, device_id_type=MESH
        )

    started = []

    def send(*args):
        cp = remote(*args)
        cp.start()
        started.append(cp)
        return cp

    lanes = lax.broadcasted_iota(jnp.int32, (GROUP, 128), 1)

    loads[0].wait()
    loads[1].wait()
    kh[...], kl[...] = split(keys[...])

    def first(which, slab):
        lh = split(lat[pl.ds(pl.multiple_of(which * HALF, HALF), HALF), :])
        s = dot3(lh, (kh[...], kl[...]), NT) * SCALE
        top = jnp.max(s, axis=1, keepdims=True)
        w = jnp.exp(s - top)
        total = jnp.sum(w, axis=1, keepdims=True)
        o = dot3(split(w), (vh[...], vl[...]), NN)
        for yy in range(NY):
            tops = jnp.zeros((GROUP, 128), F32)
            totals = jnp.zeros((GROUP, 128), F32)
            for zz in range(NZ):
                r = (zz // 4) * 128 + yy * 32 + (zz % 4) * GROUP
                tops = jnp.where(lanes == zz, top[r : r + GROUP], tops)
                totals = jnp.where(lanes == zz, total[r : r + GROUP], totals)
                for t in range(TILES):
                    slab[yy, (t * NZ + zz) * GROUP : (t * NZ + zz + 1) * GROUP, :] = o[
                        r : r + GROUP, t * 128 : (t + 1) * 128
                    ]
            slab[yy, TOP : TOP + 8, :] = tops
            slab[yy, TOP + 8 : TOP + 16, :] = totals

    loads[2].wait()
    vh[...], vl[...] = split(vals[...])
    first(1 - c, slab_send)
    pl.semaphore_wait(barrier, len(peers))
    order = (1, 3, 2, 0)
    siblings = {}
    for d in order:
        yy = lax.rem(y + d, NY)
        siblings[d] = send(slab_send.at[yy], slab_sib.at[yy], a0s.at[d], a0r.at[d], sib)
    first(c, slab_own)

    to_y = {}
    for d in order:
        yy = lax.rem(y + d, NY)
        siblings[d].wait_recv()
        mo, ms = slab_own[yy, TOP : TOP + 8, :], slab_sib[yy, TOP : TOP + 8, :]
        m = jnp.maximum(mo, ms)
        a, b = jnp.exp(mo - m), jnp.exp(ms - m)
        slab_c[d, TOP : TOP + 8, :] = m
        slab_c[d, TOP + 8 : TOP + 16, :] = (
            a * slab_own[yy, TOP + 8 : TOP + 16, :] + b * slab_sib[yy, TOP + 8 : TOP + 16, :]
        )
        for zz in range(NZ):
            az, bz = a[:, zz : zz + 1], b[:, zz : zz + 1]
            for t in range(TILES):
                r = (t * NZ + zz) * GROUP
                slab_c[d, r : r + GROUP, :] = (
                    az * slab_own[yy, r : r + GROUP, :] + bz * slab_sib[yy, r : r + GROUP, :]
                )
        if d:
            to_y[d] = send(slab_c.at[d], slab_r.at[d], a1s.at[d], a1r.at[d], ypeer(d))

    for k in (3, 4, 5):
        loads[k].wait()
    scaled = dot3(split(q[...]), split(wk[...]), NT) * (gain[...] * SCALE)
    qh[...], ql[...] = split(scaled)

    for d in (1, 3, 2):
        to_y[d].wait_recv()
    parts = [slab_c.at[0]] + [slab_r.at[d] for d in range(1, NY)]
    tops = [s[TOP : TOP + 8, :] for s in parts]
    m = functools.reduce(jnp.maximum, tops)
    scales = [jnp.exp(v - m) for v in tops]
    total = functools.reduce(jnp.add, [s * v[TOP + 8 : TOP + 16, :] for s, v in zip(scales, parts)])
    for zz in range(NZ):
        cols = [s[:, zz : zz + 1] for s in scales]
        for t in range(TILES):
            r = (t * NZ + zz) * GROUP
            piece[zz, t * GROUP : (t + 1) * GROUP, :] = functools.reduce(
                jnp.add, [u * v[r : r + GROUP, :] for u, v in zip(cols, parts)]
            )
        piece[zz, TILES * GROUP : TILES * GROUP + 8, :] = jnp.broadcast_to(m[:, zz : zz + 1], (8, 128))
        piece[zz, TILES * GROUP + 8 : PIECE, :] = jnp.broadcast_to(total[:, zz : zz + 1], (8, 128))

    z_order = (4, 3, 5, 2, 6, 1, 7)
    to_z = {}
    for d in z_order:
        zz = lax.rem(z + d, NZ)
        to_z[d] = send(piece.at[zz], piece_r.at[d], a2s.at[d], a2r.at[d], zpeer(d))
    loads[6].wait()
    wvh[...], wvl[...] = split(wv[...])
    for d in z_order:
        to_z[d].wait_recv()
    parts = [piece.at[z]] + [piece_r.at[d] for d in range(1, NZ)]
    tops = [v[TILES * GROUP : TILES * GROUP + 8, :] for v in parts]
    m = functools.reduce(jnp.maximum, tops)
    scales = [jnp.exp(v - m) for v in tops]
    total = functools.reduce(jnp.add, [s * v[TILES * GROUP + 8 : PIECE, :] for s, v in zip(scales, parts)])
    row = pl.multiple_of(c * HALF + (z // 4) * 128 + y * 32 + lax.rem(z, 4) * GROUP, GROUP)
    for t in range(TILES):
        o = functools.reduce(
            jnp.add, [s * v[t * GROUP : (t + 1) * GROUP, :] for s, v in zip(scales, parts)]
        )
        cols = slice(t * 128, (t + 1) * 128)
        g[x, pl.ds(row, GROUP), cols] = lat[pl.ds(row, GROUP), cols] + o / total

    mine = g.at[x, pl.ds(row, GROUP)]
    gather_z = {d: send(mine, mine, g1s.at[d], g1r.at[d], zpeer(d)) for d in z_order}
    for d in z_order:
        gather_z[d].wait_recv()
    low = g.at[x, pl.ds(pl.multiple_of(c * HALF + y * 32, 32), 32)]
    high = g.at[x, pl.ds(pl.multiple_of(c * HALF + 128 + y * 32, 32), 32)]
    near = (1, 3, 2)
    second = {}
    for d in near:
        second["y", d] = send(low, low, g2s.at[0, d], g2r.at[0, d], ypeer(d))
        second["x", d] = send(high, high, g2s.at[1, d], g2r.at[1, d], xpeer(d))
    for d in near:
        second["y", d].wait_recv()
        second["x", d].wait_recv()

    def low_of(xx, cc):
        return g.at[xx, pl.ds(pl.multiple_of(cc * HALF, HALF), 128)]

    def high_of(yy, cc):
        return g.at[:, pl.ds(pl.multiple_of(cc * HALF + 128 + yy * 32, 32), 32)]

    third = {}
    for d in near:
        third["x", d] = send(low_of(x, c), low_of(x, c), g3s.at[0, d], g3r.at[0, d], xpeer(d))
        third["y", d] = send(high_of(y, c), high_of(y, c), g3s.at[1, d], g3r.at[1, d], ypeer(d))

    acc[...] = jnp.zeros_like(acc)
    tot[...] = jnp.zeros_like(tot)

    def attend(blocks, start):
        n = jnp.concatenate([b.reshape(-1, D) for b in blocks], axis=0)
        n = n * (1.0 / jnp.sqrt(jnp.mean(n * n, axis=1, keepdims=True) + 1e-6))
        nh = split(n)
        s = dot3((qh[...], ql[...]), nh, NT)
        top = jnp.max(s, axis=1, keepdims=True)
        if start:
            m = top
            w = jnp.exp(s - m)
            tot[...] = jnp.broadcast_to(jnp.sum(w, axis=1, keepdims=True), tot.shape)
            acc[...] = dot3(split(w), nh, NN)
        else:
            old = mx[:, 0:1]
            m = jnp.maximum(old, top)
            w = jnp.exp(s - m)
            fade = jnp.exp(old - m)
            tot[...] = tot[...] * fade + jnp.sum(w, axis=1, keepdims=True)
            acc[...] = acc[...] * fade + dot3(split(w), nh, NN)
        mx[...] = jnp.broadcast_to(m, mx.shape)

    def source(kind, d, cc):
        if kind == "x":
            return low_of(lax.rem(x - d + NX, NX), cc)
        return high_of(lax.rem(y - d + NY, NY), cc)

    steps = [("x", 0), ("y", 0), ("x", 1), ("y", 1), ("x", 3), ("y", 3), ("x", 2), ("y", 2)]

    def forward(k):
        kind, d = steps[k]
        if d:
            third[kind, d].wait_recv()
        ref = source(kind, d, c)
        return send(ref, ref, cs.at[k], cr.at[k], sib)

    forwards = {0: forward(0), 1: forward(1)}
    for k, (kind, d) in enumerate(steps):
        if k >= 1 and k + 1 < len(steps):
            forwards[k + 1] = forward(k + 1)
        forwards[k].wait_recv()
        if k == len(steps) - 1:
            save = pltpu.make_async_copy(g.at[x], state_out, out_sem.at[0])
            save.start()
        attend([source(kind, d, 0)[...], source(kind, d, 1)[...]], k == 0)

    o = acc[...] / tot[:, 0:1] * gain[...]
    result[...] = dot3(split(o), (wvh[...], wvl[...]), NN)
    write = pltpu.make_async_copy(result, pix_out, out_sem.at[1])
    write.start()
    for cp in started:
        cp.wait_send()
    save.wait()
    write.wait()


def shards(latents, pixel_keys, pixel_values, norm_gain, w_key, w_value, pixel_queries):
    in_hbm = pl.BlockSpec(memory_space=pltpu.HBM)
    big = pltpu.VMEM((ROWS, D), F32)
    half = pltpu.VMEM((ROWS, D), BF16)
    dma = pltpu.SemaphoreType.DMA
    return pl.pallas_call(
        kernel,
        out_shape=(jax.ShapeDtypeStruct((ROWS, D), F32), jax.ShapeDtypeStruct((ROWS, D), F32)),
        in_specs=[in_hbm] * 7,
        out_specs=(in_hbm, in_hbm),
        scratch_shapes=[
            big, big, big, pltpu.VMEM((1, D), F32), big, big, big,
            half, half, half, half, half, half, half, half,
            pltpu.VMEM((NY, SLAB, 128), F32),
            pltpu.VMEM((NY, SLAB, 128), F32),
            pltpu.VMEM((NY, SLAB, 128), F32),
            pltpu.VMEM((NY, SLAB, 128), F32),
            pltpu.VMEM((NY, SLAB, 128), F32),
            pltpu.VMEM((NZ, PIECE, 128), F32),
            pltpu.VMEM((NZ, PIECE, 128), F32),
            pltpu.VMEM((NX, ROWS, D), F32),
            big,
            pltpu.VMEM((ROWS, 128), F32),
            pltpu.VMEM((ROWS, 128), F32),
            big,
            dma((7,)), dma((2,)),
            dma((NY,)), dma((NY,)), dma((NY,)), dma((NY,)),
            dma((NZ,)), dma((NZ,)), dma((NZ,)), dma((NZ,)),
            dma((2, NY)), dma((2, NY)), dma((2, NY)), dma((2, NY)),
            dma((8,)), dma((8,)),
        ],
        compiler_params=pltpu.CompilerParams(
            collective_id=0, has_side_effects=True, vmem_limit_bytes=48 << 20
        ),
        name="perceiver",
    )(latents, pixel_keys, pixel_values, norm_gain.reshape(1, D), w_key, w_value, pixel_queries)


def solution(mesh):
    in_specs = (P("lat", None), P("pix", None), P("pix", None), P(), P(), P(), P("pix", None))
    out_specs = (P("lat", None), P("pix", None))
    return jax.shard_map(shards, mesh=mesh, in_specs=in_specs, out_specs=out_specs, check_vma=False)
```

```python
import functools

import jax
import jax.numpy as jnp
from jax import lax
from jax.experimental import pallas as pl
from jax.experimental.pallas import tpu as pltpu
from jax.sharding import PartitionSpec as P

MESH = pl.DeviceIdType.MESH
F32, BF16 = jnp.float32, jnp.bfloat16
D = 512
NY, NZ, NX = 4, 8, 4
ROWS = 512
HALF = ROWS // 2
GROUP = 8
TILES = D // 128
SLAB = TILES * NZ * GROUP + 16
PIECE = TILES * GROUP + 16
TOP = TILES * NZ * GROUP
NN = (((1,), (0,)), ((), ()))
NT = (((1,), (1,)), ((), ()))
SCALE = 512.0**-0.5
BAND = 256


def split(value):
    high = value.astype(BF16)
    return high, (value - high.astype(F32)).astype(BF16)


def dot3(a, b, dims):
    def one(u, v):
        return lax.dot_general(u, v, dims, preferred_element_type=F32)

    return one(a[0], b[0]) + (one(a[0], b[1]) + one(a[1], b[0]))


def kernel(
    lat_in, keys_in, vals_in, gain_in, wk_in, wv_in, q_in, state_out, pix_out,
    lat, keys, vals, gain, wk, wv, q,
    kh, kl, vh, vl, qh, ql, wvh, wvl,
    slab_send, slab_own, slab_sib, slab_c, slab_r, piece, piece_r,
    g, acc, mx, tot,
    in_sem, out_sem, a0s, a0r, a1s, a1r, a2s, a2r, g1s, g1r, g2s, g2r, g3s, g3r, cs, cr,
):
    p = lax.axis_index("pix")
    x = lax.axis_index("lat")
    c = lax.rem(p, 2)
    y = lax.rem(p // 2, NY)
    z = p // (2 * NY)

    def at(zz, yy, cc, xx):
        return ((zz * NY + yy) * 2 + cc, xx)

    sib = at(z, y, 1 - c, x)

    def ypeer(d):
        return at(z, lax.rem(y + d + NY, NY), c, x)

    def zpeer(d):
        return at(lax.rem(z + d + NZ, NZ), y, c, x)

    def xpeer(d):
        return at(z, y, c, lax.rem(x + d + NX, NX))

    loads = []
    for k, (src, dst) in enumerate(
        [(lat_in, lat), (keys_in, keys), (vals_in, vals), (q_in, q), (wk_in, wk), (gain_in, gain), (wv_in, wv)]
    ):
        cp = pltpu.make_async_copy(src, dst, in_sem.at[k])
        cp.start()
        loads.append(cp)

    barrier = pltpu.get_barrier_semaphore()
    peers = (
        [sib]
        + [ypeer(d) for d in range(1, NY)]
        + [zpeer(d) for d in range(1, NZ)]
        + [xpeer(d) for d in range(1, NX)]
    )
    for dev in peers:
        pl.semaphore_signal(barrier, inc=1, device_id=dev, device_id_type=MESH)

    def remote(src, dst, ss, rs, dev):
        return pltpu.make_async_remote_copy(
            src_ref=src, dst_ref=dst, send_sem=ss, recv_sem=rs, device_id=dev, device_id_type=MESH
        )

    started = []

    def send(*args):
        cp = remote(*args)
        cp.start()
        started.append(cp)
        return cp

    lanes = lax.broadcasted_iota(jnp.int32, (GROUP, 128), 1)

    loads[0].wait()
    loads[1].wait()
    kh[...], kl[...] = split(keys[...])

    def first(which, slab):
        lh = split(lat[pl.ds(pl.multiple_of(which * HALF, HALF), HALF), :])
        s = dot3(lh, (kh[...], kl[...]), NT) * SCALE
        top = jnp.max(s, axis=1, keepdims=True)
        w = jnp.exp(s - top)
        total = jnp.sum(w, axis=1, keepdims=True)
        o = dot3(split(w), (vh[...], vl[...]), NN)
        for yy in range(NY):
            tops = jnp.zeros((GROUP, 128), F32)
            totals = jnp.zeros((GROUP, 128), F32)
            for zz in range(NZ):
                r = (zz // 4) * 128 + yy * 32 + (zz % 4) * GROUP
                tops = jnp.where(lanes == zz, top[r : r + GROUP], tops)
                totals = jnp.where(lanes == zz, total[r : r + GROUP], totals)
                for t in range(TILES):
                    slab[yy, (t * NZ + zz) * GROUP : (t * NZ + zz + 1) * GROUP, :] = o[
                        r : r + GROUP, t * 128 : (t + 1) * 128
                    ]
            slab[yy, TOP : TOP + 8, :] = tops
            slab[yy, TOP + 8 : TOP + 16, :] = totals

    loads[2].wait()
    vh[...], vl[...] = split(vals[...])
    first(1 - c, slab_send)
    pl.semaphore_wait(barrier, len(peers))
    order = (1, 3, 2, 0)
    siblings = {}
    for d in order:
        yy = lax.rem(y + d, NY)
        siblings[d] = send(slab_send.at[yy], slab_sib.at[yy], a0s.at[d], a0r.at[d], sib)
    first(c, slab_own)

    to_y = {}
    for d in order:
        yy = lax.rem(y + d, NY)
        siblings[d].wait_recv()
        mo, ms = slab_own[yy, TOP : TOP + 8, :], slab_sib[yy, TOP : TOP + 8, :]
        m = jnp.maximum(mo, ms)
        a, b = jnp.exp(mo - m), jnp.exp(ms - m)
        slab_c[d, TOP : TOP + 8, :] = m
        slab_c[d, TOP + 8 : TOP + 16, :] = (
            a * slab_own[yy, TOP + 8 : TOP + 16, :] + b * slab_sib[yy, TOP + 8 : TOP + 16, :]
        )
        for zz in range(NZ):
            az, bz = a[:, zz : zz + 1], b[:, zz : zz + 1]
            for t in range(TILES):
                r = (t * NZ + zz) * GROUP
                slab_c[d, r : r + GROUP, :] = (
                    az * slab_own[yy, r : r + GROUP, :] + bz * slab_sib[yy, r : r + GROUP, :]
                )
        if d:
            to_y[d] = send(slab_c.at[d], slab_r.at[d], a1s.at[d], a1r.at[d], ypeer(d))

    for k in (3, 4, 5):
        loads[k].wait()
    scaled = dot3(split(q[...]), split(wk[...]), NT) * (gain[...] * SCALE)
    qh[...], ql[...] = split(scaled)

    for d in (1, 3, 2):
        to_y[d].wait_recv()
    parts = [slab_c.at[0]] + [slab_r.at[d] for d in range(1, NY)]
    tops = [s[TOP : TOP + 8, :] for s in parts]
    m = functools.reduce(jnp.maximum, tops)
    scales = [jnp.exp(v - m) for v in tops]
    total = functools.reduce(jnp.add, [s * v[TOP + 8 : TOP + 16, :] for s, v in zip(scales, parts)])
    for zz in range(NZ):
        cols = [s[:, zz : zz + 1] for s in scales]
        for t in range(TILES):
            r = (t * NZ + zz) * GROUP
            piece[zz, t * GROUP : (t + 1) * GROUP, :] = functools.reduce(
                jnp.add, [u * v[r : r + GROUP, :] for u, v in zip(cols, parts)]
            )
        piece[zz, TILES * GROUP : TILES * GROUP + 8, :] = jnp.broadcast_to(m[:, zz : zz + 1], (8, 128))
        piece[zz, TILES * GROUP + 8 : PIECE, :] = jnp.broadcast_to(total[:, zz : zz + 1], (8, 128))

    z_order = (4, 3, 5, 2, 6, 1, 7)
    to_z = {}
    for d in z_order:
        zz = lax.rem(z + d, NZ)
        to_z[d] = send(piece.at[zz], piece_r.at[d], a2s.at[d], a2r.at[d], zpeer(d))
    loads[6].wait()
    wvh[...], wvl[...] = split(wv[...])
    for d in z_order:
        to_z[d].wait_recv()
    parts = [piece.at[z]] + [piece_r.at[d] for d in range(1, NZ)]
    tops = [v[TILES * GROUP : TILES * GROUP + 8, :] for v in parts]
    m = functools.reduce(jnp.maximum, tops)
    scales = [jnp.exp(v - m) for v in tops]
    total = functools.reduce(jnp.add, [s * v[TILES * GROUP + 8 : PIECE, :] for s, v in zip(scales, parts)])
    row = pl.multiple_of(c * HALF + (z // 4) * 128 + y * 32 + lax.rem(z, 4) * GROUP, GROUP)
    for t in range(TILES):
        o = functools.reduce(
            jnp.add, [s * v[t * GROUP : (t + 1) * GROUP, :] for s, v in zip(scales, parts)]
        )
        cols = slice(t * 128, (t + 1) * 128)
        g[x, pl.ds(row, GROUP), cols] = lat[pl.ds(row, GROUP), cols] + o / total

    mine = g.at[x, pl.ds(row, GROUP)]
    gather_z = {d: send(mine, mine, g1s.at[d], g1r.at[d], zpeer(d)) for d in z_order}
    for d in z_order:
        gather_z[d].wait_recv()
    low = g.at[x, pl.ds(pl.multiple_of(c * HALF + y * 32, 32), 32)]
    high = g.at[x, pl.ds(pl.multiple_of(c * HALF + 128 + y * 32, 32), 32)]
    near = (1, 3, 2)
    second = {}
    for d in near:
        second["y", d] = send(low, low, g2s.at[0, d], g2r.at[0, d], ypeer(d))
        second["x", d] = send(high, high, g2s.at[1, d], g2r.at[1, d], xpeer(d))
    for d in near:
        second["y", d].wait_recv()
        second["x", d].wait_recv()

    def low_of(xx, cc, part):
        first, count = {"all": (0, 128), "A": (0, 64), "B": (64, 64)}[part]
        return g.at[xx, pl.ds(pl.multiple_of(cc * HALF + first, 64), count)]

    def high_of(yy, cc, part):
        blocks = {"all": pl.ds(0, 4), "A": pl.ds(0, 2), "B": pl.ds(2, 2)}[part]
        return g.at[blocks, pl.ds(pl.multiple_of(cc * HALF + 128 + yy * 32, 32), 32)]

    def source(axis, d, cc, part):
        if axis == "x":
            return low_of(lax.rem(x - d + NX, NX), cc, part)
        return high_of(lax.rem(y - d + NY, NY), cc, part)

    slots = {}
    for axis in "xy":
        for d, part in ((1, "A"), (3, "B"), (1, "B"), (3, "A"), (2, "A"), (2, "B")):
            slots[axis, d, part] = len(slots)
    third = {}

    def push(axis, back, d, part):
        step = (d - back) % 4
        k = slots[axis, d, part]
        ref = source(axis, back, c, part)
        third[axis, d, part] = send(
            ref, ref, g3s.at[k], g3r.at[k], xpeer(step) if axis == "x" else ypeer(step)
        )

    for d, part in ((1, "A"), (3, "B"), (1, "B"), (3, "A")):
        for axis in "xy":
            push(axis, 0, d, part)

    def wide(value, times):
        return jnp.concatenate([value] * times, axis=1)

    def attend(blocks, start):
        n = jnp.concatenate([b.reshape(-1, D) for b in blocks], axis=0)
        n = n * (1.0 / jnp.sqrt(jnp.mean(n * n, axis=1, keepdims=True) + 1e-6))
        nh = split(n)
        bands = [slice(r, r + BAND) for r in range(0, ROWS, BAND)]

        def scores(band):
            return dot3((qh[band, :], ql[band, :]), nh, NT)

        ahead = scores(bands[0])
        for k, band in enumerate(bands):
            s = ahead
            if k + 1 < len(bands):
                ahead = scores(bands[k + 1])
            columns = s.shape[1] // 128
            top = jnp.broadcast_to(jnp.max(s, axis=1, keepdims=True), (BAND, 128))
            m = top if start else jnp.maximum(mx[band, :], top)
            w = jnp.exp(s - wide(m, columns))
            total = functools.reduce(jnp.add, [w[:, t * 128 : (t + 1) * 128] for t in range(columns)])
            read = dot3(split(w), nh, NN)
            if not start:
                fade = jnp.exp(mx[band, :] - m)
                total = tot[band, :] * fade + total
                read = acc[band, :] * wide(fade, TILES) + read
            mx[band, :] = m
            tot[band, :] = total
            acc[band, :] = read

    chunks = [
        [("x", 0, "all"), ("y", 0, "all")],
        [("x", 1, "A"), ("y", 1, "A"), ("x", 3, "B"), ("y", 3, "B")],
        [("x", 1, "B"), ("y", 1, "B"), ("x", 3, "A"), ("y", 3, "A")],
        [("x", 2, "A"), ("x", 2, "B"), ("y", 2, "A"), ("y", 2, "B")],
    ]
    passed = {}

    def pass_on(chunk):
        for axis, d, part in chunk:
            if d:
                third[axis, d, part].wait_recv()
            if (d, part) == (1, "A"):
                push(axis, 1, 2, "A")
            if (d, part) == (3, "B"):
                push(axis, 3, 2, "B")
            ref = source(axis, d, c, part)
            k = len(passed)
            passed[axis, d, part] = send(ref, ref, cs.at[k], cr.at[k], sib)

    def use(chunk, start=False):
        for item in chunk:
            passed[item].wait_recv()
        attend([source(axis, d, cc, part)[...] for axis, d, part in chunk for cc in range(2)], start)

    pass_on(chunks[0])
    use(chunks[0], True)
    pass_on(chunks[1])
    pass_on(chunks[2])
    use(chunks[1])
    use(chunks[2])
    pass_on(chunks[3])
    for item in chunks[3]:
        passed[item].wait_recv()
    save = pltpu.make_async_copy(g.at[x], state_out, out_sem.at[0])
    save.start()
    attend([source(axis, d, cc, part)[...] for axis, d, part in chunks[3] for cc in range(2)], False)

    o = acc[...] / jnp.sum(tot[...], axis=1, keepdims=True) * gain[...]
    pix_out[...] = dot3(split(o), (wvh[...], wvl[...]), NN)
    for cp in started:
        cp.wait_send()
    save.wait()


def shards(latents, pixel_keys, pixel_values, norm_gain, w_key, w_value, pixel_queries):
    in_hbm = pl.BlockSpec(memory_space=pltpu.HBM)
    big = pltpu.VMEM((ROWS, D), F32)
    half = pltpu.VMEM((ROWS, D), BF16)
    dma = pltpu.SemaphoreType.DMA
    return pl.pallas_call(
        kernel,
        out_shape=(jax.ShapeDtypeStruct((ROWS, D), F32), jax.ShapeDtypeStruct((ROWS, D), F32)),
        in_specs=[in_hbm] * 7,
        out_specs=(pl.BlockSpec(memory_space=pltpu.VMEM),) * 2,
        scratch_shapes=[
            big, big, big, pltpu.VMEM((1, D), F32), big, big, big,
            half, half, half, half, half, half, half, half,
            pltpu.VMEM((NY, SLAB, 128), F32),
            pltpu.VMEM((NY, SLAB, 128), F32),
            pltpu.VMEM((NY, SLAB, 128), F32),
            pltpu.VMEM((NY, SLAB, 128), F32),
            pltpu.VMEM((NY, SLAB, 128), F32),
            pltpu.VMEM((NZ, PIECE, 128), F32),
            pltpu.VMEM((NZ, PIECE, 128), F32),
            pltpu.VMEM((NX, ROWS, D), F32),
            big,
            pltpu.VMEM((ROWS, 128), F32),
            pltpu.VMEM((ROWS, 128), F32),
            dma((7,)), dma((1,)),
            dma((NY,)), dma((NY,)), dma((NY,)), dma((NY,)),
            dma((NZ,)), dma((NZ,)), dma((NZ,)), dma((NZ,)),
            dma((2, NY)), dma((2, NY)), dma((12,)), dma((12,)),
            dma((14,)), dma((14,)),
        ],
        compiler_params=pltpu.CompilerParams(
            collective_id=0, has_side_effects=True, vmem_limit_bytes=60 << 20
        ),
        name="perceiver",
    )(latents, pixel_keys, pixel_values, norm_gain.reshape(1, D), w_key, w_value, pixel_queries)


def solution(mesh):
    in_specs = (P("lat", None), P("pix", None), P("pix", None), P(), P(), P(), P("pix", None))
    out_specs = (P("lat", None), P("pix", None))
    return jax.shard_map(shards, mesh=mesh, in_specs=in_specs, out_specs=out_specs, check_vma=False)
```

```python
import functools

import jax
import jax.numpy as jnp
from jax import lax
from jax.experimental import pallas as pl
from jax.experimental.pallas import tpu as pltpu
from jax.sharding import PartitionSpec as P

MESH = pl.DeviceIdType.MESH
F32, BF16 = jnp.float32, jnp.bfloat16
D = 512
NY, NZ, NX = 4, 8, 4
ROWS = 512
HALF = ROWS // 2
GROUP = 8
TILES = D // 128
SLAB = TILES * NZ * GROUP + 16
PIECE = TILES * GROUP + 8
TOP = TILES * NZ * GROUP
NN = (((1,), (0,)), ((), ()))
NT = (((1,), (1,)), ((), ()))
SCALE = 512.0**-0.5
BAND = 256


def split(value):
    high = value.astype(BF16)
    return high, (value - high.astype(F32)).astype(BF16)


def dot3(a, b, dims):
    def one(u, v):
        return lax.dot_general(u, v, dims, preferred_element_type=F32)

    return one(a[0], b[0]) + (one(a[0], b[1]) + one(a[1], b[0]))


def kernel(
    lat_in, keys_in, vals_in, gain_in, wk_in, wv_in, q_in, state_out, pix_out,
    lat, keys, vals, gain, wk, wv, q,
    kh, kl, vh, vl, qh, ql, wvh, wvl,
    slab_send, slab_own, slab_sib, slab_c, slab_r, piece, piece_r,
    g, acc, mx, tot,
    in_sem, out_sem, a0s, a0r, a1s, a1r, a2s, a2r, g1s, g1r, g2s, g2r, g3s, g3r, cs, cr,
):
    p = lax.axis_index("pix")
    x = lax.axis_index("lat")
    c = lax.rem(p, 2)
    y = lax.rem(p // 2, NY)
    z = p // (2 * NY)

    def at(zz, yy, cc, xx):
        return ((zz * NY + yy) * 2 + cc, xx)

    sib = at(z, y, 1 - c, x)

    def ypeer(d):
        return at(z, lax.rem(y + d + NY, NY), c, x)

    def zpeer(d):
        return at(lax.rem(z + d + NZ, NZ), y, c, x)

    def xpeer(d):
        return at(z, y, c, lax.rem(x + d + NX, NX))

    loads = []
    for k, (src, dst) in enumerate(
        [(lat_in, lat), (keys_in, keys), (vals_in, vals), (q_in, q), (wk_in, wk), (gain_in, gain), (wv_in, wv)]
    ):
        cp = pltpu.make_async_copy(src, dst, in_sem.at[k])
        cp.start()
        loads.append(cp)

    barrier = pltpu.get_barrier_semaphore()
    peers = (
        [sib]
        + [ypeer(d) for d in range(1, NY)]
        + [zpeer(d) for d in range(1, NZ)]
        + [xpeer(d) for d in range(1, NX)]
    )
    for dev in peers:
        pl.semaphore_signal(barrier, inc=1, device_id=dev, device_id_type=MESH)

    def remote(src, dst, ss, rs, dev):
        return pltpu.make_async_remote_copy(
            src_ref=src, dst_ref=dst, send_sem=ss, recv_sem=rs, device_id=dev, device_id_type=MESH
        )

    started = []

    def send(*args):
        cp = remote(*args)
        cp.start()
        started.append(cp)
        return cp

    lanes = lax.broadcasted_iota(jnp.int32, (GROUP, 128), 1)

    loads[0].wait()
    loads[1].wait()
    kh[...], kl[...] = split(keys[...])

    def first_scores(which):
        lh = split(lat[pl.ds(pl.multiple_of(which * HALF, HALF), HALF), :])
        return dot3(lh, (kh[...], kl[...]), NT) * SCALE

    def first_read(s, slab):
        top = jnp.max(s, axis=1, keepdims=True)
        w = jnp.exp(s - top)
        total = jnp.sum(w, axis=1, keepdims=True)
        o = dot3(split(w), (vh[...], vl[...]), NN)
        for yy in range(NY):
            tops = jnp.zeros((GROUP, 128), F32)
            totals = jnp.zeros((GROUP, 128), F32)
            for zz in range(NZ):
                r = (zz // 4) * 128 + yy * 32 + (zz % 4) * GROUP
                tops = jnp.where(lanes == zz, top[r : r + GROUP], tops)
                totals = jnp.where(lanes == zz, total[r : r + GROUP], totals)
                for t in range(TILES):
                    slab[yy, (t * NZ + zz) * GROUP : (t * NZ + zz + 1) * GROUP, :] = o[
                        r : r + GROUP, t * 128 : (t + 1) * 128
                    ]
            slab[yy, TOP : TOP + 8, :] = tops
            slab[yy, TOP + 8 : TOP + 16, :] = totals

    away = first_scores(1 - c)
    loads[2].wait()
    vh[...], vl[...] = split(vals[...])
    here = first_scores(c)
    first_read(away, slab_send)
    pl.semaphore_wait(barrier, len(peers))
    order = (2, 1, 3, 0)
    siblings = {}
    for d in order:
        yy = lax.rem(y + d, NY)
        siblings[d] = send(slab_send.at[yy], slab_sib.at[yy], a0s.at[d], a0r.at[d], sib)
    first_read(here, slab_own)

    to_y = {}
    for d in order:
        yy = lax.rem(y + d, NY)
        siblings[d].wait_recv()
        mo, ms = slab_own[yy, TOP : TOP + 8, :], slab_sib[yy, TOP : TOP + 8, :]
        m = jnp.maximum(mo, ms)
        a, b = jnp.exp(mo - m), jnp.exp(ms - m)
        slab_c[d, TOP : TOP + 8, :] = m
        slab_c[d, TOP + 8 : TOP + 16, :] = (
            a * slab_own[yy, TOP + 8 : TOP + 16, :] + b * slab_sib[yy, TOP + 8 : TOP + 16, :]
        )
        for zz in range(NZ):
            az, bz = a[:, zz : zz + 1], b[:, zz : zz + 1]
            for t in range(TILES):
                r = (t * NZ + zz) * GROUP
                slab_c[d, r : r + GROUP, :] = (
                    az * slab_own[yy, r : r + GROUP, :] + bz * slab_sib[yy, r : r + GROUP, :]
                )
        if d:
            to_y[d] = send(slab_c.at[d], slab_r.at[d], a1s.at[d], a1r.at[d], ypeer(d))

    for k in (3, 4, 5):
        loads[k].wait()
    scaled = dot3(split(q[...]), split(wk[...]), NT) * (gain[...] * SCALE)
    qh[...], ql[...] = split(scaled)

    for d in (1, 3, 2):
        to_y[d].wait_recv()
    parts = [slab_c.at[0]] + [slab_r.at[d] for d in range(1, NY)]
    tops = [s[TOP : TOP + 8, :] for s in parts]
    m = functools.reduce(jnp.maximum, tops)
    scales = [jnp.exp(v - m) for v in tops]
    total = functools.reduce(jnp.add, [s * v[TOP + 8 : TOP + 16, :] for s, v in zip(scales, parts)])
    for zz in range(NZ):
        cols = [s[:, zz : zz + 1] for s in scales]
        for t in range(TILES):
            r = (t * NZ + zz) * GROUP
            piece[zz, t * GROUP : (t + 1) * GROUP, :] = functools.reduce(
                jnp.add, [u * v[r : r + GROUP, :] for u, v in zip(cols, parts)]
            )
        piece[zz, TILES * GROUP : PIECE, :] = jnp.where(lanes < 64, m[:, zz : zz + 1], total[:, zz : zz + 1])

    z_order = (4, 3, 5, 2, 6, 1, 7)
    to_z = {}
    for d in z_order:
        zz = lax.rem(z + d, NZ)
        to_z[d] = send(piece.at[zz], piece_r.at[d], a2s.at[d], a2r.at[d], zpeer(d))
    loads[6].wait()
    wvh[...], wvl[...] = split(wv[...])
    for d in z_order:
        to_z[d].wait_recv()
    parts = [piece.at[z]] + [piece_r.at[d] for d in range(1, NZ)]
    stats = [v[TILES * GROUP : PIECE, :] for v in parts]
    tops = [v[:, 0:1] for v in stats]
    m = functools.reduce(jnp.maximum, tops)
    scales = [jnp.exp(v - m) for v in tops]
    total = functools.reduce(jnp.add, [s * v[:, 64:65] for s, v in zip(scales, stats)])
    row = pl.multiple_of(c * HALF + (z // 4) * 128 + y * 32 + lax.rem(z, 4) * GROUP, GROUP)
    for t in range(TILES):
        o = functools.reduce(
            jnp.add, [s * v[t * GROUP : (t + 1) * GROUP, :] for s, v in zip(scales, parts)]
        )
        cols = slice(t * 128, (t + 1) * 128)
        g[x, pl.ds(row, GROUP), cols] = lat[pl.ds(row, GROUP), cols] + o / total

    mine = g.at[x, pl.ds(row, GROUP)]
    gather_z = {d: send(mine, mine, g1s.at[d], g1r.at[d], zpeer(d)) for d in z_order}
    for d in z_order:
        gather_z[d].wait_recv()
    low = g.at[x, pl.ds(pl.multiple_of(c * HALF + y * 32, 32), 32)]
    high = g.at[x, pl.ds(pl.multiple_of(c * HALF + 128 + y * 32, 32), 32)]
    near = (1, 3, 2)
    second = {}
    for d in near:
        second["y", d] = send(low, low, g2s.at[0, d], g2r.at[0, d], ypeer(d))
        second["x", d] = send(high, high, g2s.at[1, d], g2r.at[1, d], xpeer(d))

    def low_of(xx, cc, part):
        first, count = {"all": (0, 128), "A": (0, 64), "B": (64, 64)}[part]
        return g.at[xx, pl.ds(pl.multiple_of(cc * HALF + first, 64), count)]

    def high_of(yy, cc, part):
        blocks = {"all": pl.ds(0, 4), "A": pl.ds(0, 2), "B": pl.ds(2, 2)}[part]
        return g.at[blocks, pl.ds(pl.multiple_of(cc * HALF + 128 + yy * 32, 32), 32)]

    def source(axis, d, cc, part):
        if axis == "x":
            return low_of(lax.rem(x - d + NX, NX), cc, part)
        return high_of(lax.rem(y - d + NY, NY), cc, part)

    slots = {}
    for axis in "xy":
        for d, part in ((1, "A"), (3, "B"), (1, "B"), (3, "A"), (2, "A"), (2, "B")):
            slots[axis, d, part] = len(slots)
    third = {}

    def push(axis, back, d, part):
        step = (d - back) % 4
        k = slots[axis, d, part]
        ref = source(axis, back, c, part)
        third[axis, d, part] = send(
            ref, ref, g3s.at[k], g3r.at[k], xpeer(step) if axis == "x" else ypeer(step)
        )

    earlier = len(started)
    for axis, before in (("x", "y"), ("y", "x")):
        for d in near:
            second[before, d].wait_recv()
        for d, part in ((1, "A"), (3, "B"), (1, "B"), (3, "A")):
            push(axis, 0, d, part)

    def wide(value, times):
        return jnp.concatenate([value] * times, axis=1)

    def attend(chunk, start=False, last=False):
        blocks = [source(axis, d, cc, part)[...] for axis, d, part in chunk for cc in range(2)]
        n = jnp.concatenate([b.reshape(-1, D) for b in blocks], axis=0)
        n = n * (1.0 / jnp.sqrt(jnp.mean(n * n, axis=1, keepdims=True) + 1e-6))
        nh = split(n)
        bands = [slice(r, r + BAND) for r in range(0, ROWS, BAND)]

        def scores(band):
            return dot3((qh[band, :], ql[band, :]), nh, NT)

        ahead = scores(bands[0])
        for k, band in enumerate(bands):
            s = ahead
            if k + 1 < len(bands):
                ahead = scores(bands[k + 1])
            columns = s.shape[1] // 128
            top = jnp.broadcast_to(jnp.max(s, axis=1, keepdims=True), (BAND, 128))
            m = top if start else jnp.maximum(mx[band, :], top)
            w = jnp.exp(s - wide(m, columns))
            total = functools.reduce(jnp.add, [w[:, t * 128 : (t + 1) * 128] for t in range(columns)])
            read = dot3(split(w), nh, NN)
            if not start:
                fade = jnp.exp(mx[band, :] - m)
                total = tot[band, :] * fade + total
                read = acc[band, :] * wide(fade, TILES) + read
            if last:
                o = read / jnp.sum(total, axis=1, keepdims=True) * gain[...]
                pix_out[band, :] = dot3(split(o), (wvh[...], wvl[...]), NN)
            else:
                mx[band, :] = m
                tot[band, :] = total
                acc[band, :] = read

    chunks = [
        [("x", 0, "all"), ("y", 0, "all")],
        [("x", 1, "A"), ("y", 1, "A"), ("x", 3, "B"), ("y", 3, "B")],
        [("x", 1, "B"), ("y", 1, "B"), ("x", 3, "A"), ("y", 3, "A")],
        [("x", 2, "A"), ("x", 2, "B"), ("y", 2, "A"), ("y", 2, "B")],
    ]
    passed = {}

    def pass_on(chunk):
        for axis, d, part in chunk:
            if d:
                third[axis, d, part].wait_recv()
            if (d, part) == (1, "A"):
                push(axis, 1, 2, "A")
            if (d, part) == (3, "B"):
                push(axis, 3, 2, "B")
            ref = source(axis, d, c, part)
            k = len(passed)
            passed[axis, d, part] = send(ref, ref, cs.at[k], cr.at[k], sib)

    def wait_for(chunk):
        for item in chunk:
            passed[item].wait_recv()

    pass_on(chunks[0])
    wait_for(chunks[0])
    attend(chunks[0], start=True)
    for cp in started[:earlier]:
        cp.wait_send()
    pass_on(chunks[1])
    pass_on(chunks[2])
    sent = len(started)
    wait_for(chunks[1])
    attend(chunks[1])
    wait_for(chunks[2])
    attend(chunks[2])
    for cp in started[earlier:sent]:
        cp.wait_send()
    pass_on(chunks[3])
    wait_for(chunks[3])
    save = pltpu.make_async_copy(g.at[x], state_out, out_sem.at[0])
    save.start()
    attend(chunks[3], last=True)
    for cp in started[sent:]:
        cp.wait_send()
    save.wait()


def shards(latents, pixel_keys, pixel_values, norm_gain, w_key, w_value, pixel_queries):
    operands = (latents, pixel_keys, pixel_values, norm_gain.reshape(1, D), w_key, w_value, pixel_queries)
    in_hbm = pl.BlockSpec(memory_space=pltpu.HBM)
    big = pltpu.VMEM((ROWS, D), F32)
    half = pltpu.VMEM((ROWS, D), BF16)
    dma = pltpu.SemaphoreType.DMA
    return pl.pallas_call(
        kernel,
        out_shape=(jax.ShapeDtypeStruct((ROWS, D), F32), jax.ShapeDtypeStruct((ROWS, D), F32)),
        in_specs=[in_hbm] * 7,
        out_specs=(pl.BlockSpec(memory_space=pltpu.VMEM),) * 2,
        scratch_shapes=[
            big, big, big, pltpu.VMEM((1, D), F32), big, big, big,
            half, half, half, half, half, half, half, half,
            pltpu.VMEM((NY, SLAB, 128), F32),
            pltpu.VMEM((NY, SLAB, 128), F32),
            pltpu.VMEM((NY, SLAB, 128), F32),
            pltpu.VMEM((NY, SLAB, 128), F32),
            pltpu.VMEM((NY, SLAB, 128), F32),
            pltpu.VMEM((NZ, PIECE, 128), F32),
            pltpu.VMEM((NZ, PIECE, 128), F32),
            pltpu.VMEM((NX, ROWS, D), F32),
            big,
            pltpu.VMEM((ROWS, 128), F32),
            pltpu.VMEM((ROWS, 128), F32),
            dma((7,)), dma((1,)),
            dma((NY,)), dma((NY,)), dma((NY,)), dma((NY,)),
            dma((NZ,)), dma((NZ,)), dma((NZ,)), dma((NZ,)),
            dma((2, NY)), dma((2, NY)), dma((12,)), dma((12,)),
            dma((14,)), dma((14,)),
        ],
        compiler_params=pltpu.CompilerParams(
            collective_id=0, has_side_effects=True, vmem_limit_bytes=50 << 20
        ),
        name="perceiver",
    )(*(pltpu.with_memory_space_constraint(v, pltpu.HBM) for v in operands))


def solution(mesh):
    in_specs = (P("lat", None), P("pix", None), P("pix", None), P(), P(), P(), P("pix", None))
    out_specs = (P("lat", None), P("pix", None))
    return jax.shard_map(shards, mesh=mesh, in_specs=in_specs, out_specs=out_specs, check_vma=False)
```

```python
import functools

import jax
import jax.numpy as jnp
from jax import lax
from jax.experimental import pallas as pl
from jax.experimental.pallas import tpu as pltpu
from jax.sharding import PartitionSpec as P

MESH = pl.DeviceIdType.MESH
F32, BF16 = jnp.float32, jnp.bfloat16
D = 512
NY, NZ, NX = 4, 8, 4
ROWS = 512
HALF = ROWS // 2
GROUP = 8
TILES = D // 128
SLAB = TILES * NZ * GROUP + 16
PIECE = TILES * GROUP + 8
TOP = TILES * NZ * GROUP
NN = (((1,), (0,)), ((), ()))
NT = (((1,), (1,)), ((), ()))
SCALE = 512.0**-0.5
BAND = 256


def split(value):
    high = value.astype(BF16)
    return high, (value - high.astype(F32)).astype(BF16)


def dot3(a, b, dims):
    def one(u, v):
        return lax.dot_general(u, v, dims, preferred_element_type=F32)

    return one(a[0], b[0]) + (one(a[0], b[1]) + one(a[1], b[0]))


def kernel(
    lat_in, keys_in, vals_in, gain_in, wk_in, wv_in, q_in, state_out, read_out, wvh, wvl,
    lat, keys, vals, gain, wk, wv, q,
    kh, kl, vh, vl, qh, ql,
    slab_send, slab_own, slab_sib, slab_c, slab_r, piece, piece_r,
    g, acc, mx, tot,
    in_sem, out_sem, a0s, a0r, a1s, a1r, a2s, a2r, g1s, g1r, g2s, g2r, g3s, g3r, cs, cr,
):
    p = lax.axis_index("pix")
    x = lax.axis_index("lat")
    c = lax.rem(p, 2)
    y = lax.rem(p // 2, NY)
    z = p // (2 * NY)

    def at(zz, yy, cc, xx):
        return ((zz * NY + yy) * 2 + cc, xx)

    sib = at(z, y, 1 - c, x)

    def ypeer(d):
        return at(z, lax.rem(y + d + NY, NY), c, x)

    def zpeer(d):
        return at(lax.rem(z + d + NZ, NZ), y, c, x)

    def xpeer(d):
        return at(z, y, c, lax.rem(x + d + NX, NX))

    loads = []
    for k, (src, dst) in enumerate(
        [(lat_in, lat), (keys_in, keys), (vals_in, vals), (q_in, q), (wk_in, wk), (gain_in, gain), (wv_in, wv)]
    ):
        loads.append(pltpu.make_async_copy(src, dst, in_sem.at[k]))
    for cp in loads[:3]:
        cp.start()

    barrier = pltpu.get_barrier_semaphore()
    peers = (
        [sib]
        + [ypeer(d) for d in range(1, NY)]
        + [zpeer(d) for d in range(1, NZ)]
        + [xpeer(d) for d in range(1, NX)]
    )
    for dev in peers:
        pl.semaphore_signal(barrier, inc=1, device_id=dev, device_id_type=MESH)

    def remote(src, dst, ss, rs, dev):
        return pltpu.make_async_remote_copy(
            src_ref=src, dst_ref=dst, send_sem=ss, recv_sem=rs, device_id=dev, device_id_type=MESH
        )

    started = []

    def send(*args, keep=True):
        cp = remote(*args)
        cp.start()
        if keep:
            started.append(cp)
        return cp

    lanes = lax.broadcasted_iota(jnp.int32, (GROUP, 128), 1)

    loads[0].wait()
    loads[1].wait()
    kh[...], kl[...] = split(keys[...])

    def first_scores(which):
        lh = split(lat[pl.ds(pl.multiple_of(which * HALF, HALF), HALF), :])
        return dot3(lh, (kh[...], kl[...]), NT) * SCALE

    def first_read(s, slab):
        top = jnp.max(s, axis=1, keepdims=True)
        w = jnp.exp(s - top)
        total = jnp.sum(w, axis=1, keepdims=True)
        o = dot3(split(w), (vh[...], vl[...]), NN)
        for yy in range(NY):
            tops = jnp.zeros((GROUP, 128), F32)
            totals = jnp.zeros((GROUP, 128), F32)
            for zz in range(NZ):
                r = (zz // 4) * 128 + yy * 32 + (zz % 4) * GROUP
                tops = jnp.where(lanes == zz, top[r : r + GROUP], tops)
                totals = jnp.where(lanes == zz, total[r : r + GROUP], totals)
                for t in range(TILES):
                    slab[yy, (t * NZ + zz) * GROUP : (t * NZ + zz + 1) * GROUP, :] = o[
                        r : r + GROUP, t * 128 : (t + 1) * 128
                    ]
            slab[yy, TOP : TOP + 8, :] = tops
            slab[yy, TOP + 8 : TOP + 16, :] = totals

    away = first_scores(1 - c)
    loads[2].wait()
    for cp in loads[3:]:
        cp.start()
    vh[...], vl[...] = split(vals[...])
    here = first_scores(c)
    first_read(away, slab_send)
    pl.semaphore_wait(barrier, len(peers))
    order = (2, 1, 3, 0)
    siblings = {}
    for d in order:
        yy = lax.rem(y + d, NY)
        siblings[d] = send(slab_send.at[yy], slab_sib.at[yy], a0s.at[d], a0r.at[d], sib)
    first_read(here, slab_own)

    to_y = {}
    for d in order:
        yy = lax.rem(y + d, NY)
        siblings[d].wait_recv()
        mo, ms = slab_own[yy, TOP : TOP + 8, :], slab_sib[yy, TOP : TOP + 8, :]
        m = jnp.maximum(mo, ms)
        a, b = jnp.exp(mo - m), jnp.exp(ms - m)
        slab_c[d, TOP : TOP + 8, :] = m
        slab_c[d, TOP + 8 : TOP + 16, :] = (
            a * slab_own[yy, TOP + 8 : TOP + 16, :] + b * slab_sib[yy, TOP + 8 : TOP + 16, :]
        )
        for zz in range(NZ):
            az, bz = a[:, zz : zz + 1], b[:, zz : zz + 1]
            for t in range(TILES):
                r = (t * NZ + zz) * GROUP
                slab_c[d, r : r + GROUP, :] = (
                    az * slab_own[yy, r : r + GROUP, :] + bz * slab_sib[yy, r : r + GROUP, :]
                )
        if d:
            to_y[d] = send(slab_c.at[d], slab_r.at[d], a1s.at[d], a1r.at[d], ypeer(d))

    for k in (3, 4, 5):
        loads[k].wait()
    scaled = dot3(split(q[...]), split(wk[...]), NT) * (gain[...] * SCALE)
    qh[...], ql[...] = split(scaled)

    for d in (1, 3, 2):
        to_y[d].wait_recv()
    parts = [slab_c.at[0]] + [slab_r.at[d] for d in range(1, NY)]
    tops = [s[TOP : TOP + 8, :] for s in parts]
    m = functools.reduce(jnp.maximum, tops)
    scales = [jnp.exp(v - m) for v in tops]
    total = functools.reduce(jnp.add, [s * v[TOP + 8 : TOP + 16, :] for s, v in zip(scales, parts)])
    for zz in range(NZ):
        cols = [s[:, zz : zz + 1] for s in scales]
        for t in range(TILES):
            r = (t * NZ + zz) * GROUP
            piece[zz, t * GROUP : (t + 1) * GROUP, :] = functools.reduce(
                jnp.add, [u * v[r : r + GROUP, :] for u, v in zip(cols, parts)]
            )
        piece[zz, TILES * GROUP : PIECE, :] = jnp.where(lanes < 64, m[:, zz : zz + 1], total[:, zz : zz + 1])

    z_order = (4, 3, 5, 2, 6, 1, 7)
    to_z = {}
    for d in z_order:
        zz = lax.rem(z + d, NZ)
        to_z[d] = send(piece.at[zz], piece_r.at[d], a2s.at[d], a2r.at[d], zpeer(d))
    loads[6].wait()
    wvh[...], wvl[...] = split(wv[...])
    for d in z_order:
        to_z[d].wait_recv()
    parts = [piece.at[z]] + [piece_r.at[d] for d in range(1, NZ)]
    stats = [v[TILES * GROUP : PIECE, :] for v in parts]
    tops = [v[:, 0:1] for v in stats]
    m = functools.reduce(jnp.maximum, tops)
    scales = [jnp.exp(v - m) for v in tops]
    total = functools.reduce(jnp.add, [s * v[:, 64:65] for s, v in zip(scales, stats)])
    row = pl.multiple_of(c * HALF + (z // 4) * 128 + y * 32 + lax.rem(z, 4) * GROUP, GROUP)
    for t in range(TILES):
        o = functools.reduce(
            jnp.add, [s * v[t * GROUP : (t + 1) * GROUP, :] for s, v in zip(scales, parts)]
        )
        cols = slice(t * 128, (t + 1) * 128)
        g[x, pl.ds(row, GROUP), cols] = lat[pl.ds(row, GROUP), cols] + o / total

    mine = g.at[x, pl.ds(row, GROUP)]
    gather_z = {d: send(mine, mine, g1s.at[d], g1r.at[d], zpeer(d)) for d in z_order}
    for d in z_order:
        gather_z[d].wait_recv()
    low = g.at[x, pl.ds(pl.multiple_of(c * HALF + y * 32, 32), 32)]
    high = g.at[x, pl.ds(pl.multiple_of(c * HALF + 128 + y * 32, 32), 32)]
    near = (1, 3, 2)
    second = {}
    for d in near:
        second["y", d] = send(low, low, g2s.at[0, d], g2r.at[0, d], ypeer(d))
        second["x", d] = send(high, high, g2s.at[1, d], g2r.at[1, d], xpeer(d))

    def low_of(xx, cc, part):
        first, count = {"all": (0, 128), "A": (0, 64), "B": (64, 64)}[part]
        return g.at[xx, pl.ds(pl.multiple_of(cc * HALF + first, 64), count)]

    def high_of(yy, cc, part):
        blocks = {"all": pl.ds(0, 4), "A": pl.ds(0, 2), "B": pl.ds(2, 2)}[part]
        return g.at[blocks, pl.ds(pl.multiple_of(cc * HALF + 128 + yy * 32, 32), 32)]

    def source(axis, d, cc, part):
        if axis == "x":
            return low_of(lax.rem(x - d + NX, NX), cc, part)
        return high_of(lax.rem(y - d + NY, NY), cc, part)

    slots = {}
    for axis in "xy":
        for d, part in ((1, "A"), (3, "B"), (1, "B"), (3, "A"), (2, "A"), (2, "B")):
            slots[axis, d, part] = len(slots)
    third = {}

    def push(axis, back, d, part):
        step = (d - back) % 4
        k = slots[axis, d, part]
        ref = source(axis, back, c, part)
        third[axis, d, part] = send(
            ref, ref, g3s.at[k], g3r.at[k], xpeer(step) if axis == "x" else ypeer(step),
        )

    earlier = len(started)
    for axis, before in (("x", "y"), ("y", "x")):
        for d in near:
            second[before, d].wait_recv()
        for d, part in ((1, "A"), (3, "B"), (1, "B"), (3, "A")):
            push(axis, 0, d, part)

    def wide(value, times):
        return jnp.concatenate([value] * times, axis=1)

    def attend(chunk, start=False, last=False):
        blocks = [source(axis, d, cc, part)[...] for axis, d, part in chunk for cc in range(2)]
        n = jnp.concatenate([b.reshape(-1, D) for b in blocks], axis=0)
        n = n * (1.0 / jnp.sqrt(jnp.mean(n * n, axis=1, keepdims=True) + 1e-6))
        nh = split(n)
        bands = [slice(r, r + BAND) for r in range(0, ROWS, BAND)]

        def scores(band):
            return dot3((qh[band, :], ql[band, :]), nh, NT)

        ahead = scores(bands[0])
        for k, band in enumerate(bands):
            s = ahead
            if k + 1 < len(bands):
                ahead = scores(bands[k + 1])
            columns = s.shape[1] // 128
            top = jnp.broadcast_to(jnp.max(s, axis=1, keepdims=True), (BAND, 128))
            m = top if start else jnp.maximum(mx[band, :], top)
            w = jnp.exp(s - wide(m, columns))
            total = functools.reduce(jnp.add, [w[:, t * 128 : (t + 1) * 128] for t in range(columns)])
            read = dot3(split(w), nh, NN)
            if not start:
                fade = jnp.exp(mx[band, :] - m)
                total = tot[band, :] * fade + total
                read = acc[band, :] * wide(fade, TILES) + read
            if last:
                read_out[band, :] = read / jnp.sum(total, axis=1, keepdims=True) * gain[...]
            else:
                mx[band, :] = m
                tot[band, :] = total
                acc[band, :] = read

    chunks = [
        [("x", 0, "all"), ("y", 0, "all")],
        [("x", 1, "A"), ("y", 1, "A"), ("x", 3, "B"), ("y", 3, "B")],
        [("x", 1, "B"), ("y", 1, "B"), ("x", 3, "A"), ("y", 3, "A")],
        [("x", 2, "A"), ("x", 2, "B"), ("y", 2, "A"), ("y", 2, "B")],
    ]
    passed = {}

    def pass_on(chunk):
        for axis, d, part in chunk:
            if d:
                third[axis, d, part].wait_recv()
            if (d, part) == (1, "A"):
                push(axis, 1, 2, "A")
            if (d, part) == (3, "B"):
                push(axis, 3, 2, "B")
            ref = source(axis, d, c, part)
            k = len(passed)
            passed[axis, d, part] = send(ref, ref, cs.at[k], cr.at[k], sib)

    def wait_for(chunk):
        for item in chunk:
            passed[item].wait_recv()

    pass_on(chunks[0])
    wait_for(chunks[0])
    attend(chunks[0], start=True)
    for cp in started[:earlier]:
        cp.wait_send()
    pass_on(chunks[1])
    pass_on(chunks[2])
    sent = len(started)
    wait_for(chunks[1])
    attend(chunks[1])
    pass_on(chunks[3])
    wait_for(chunks[2])
    attend(chunks[2])
    for cp in started[earlier:sent]:
        cp.wait_send()
    wait_for(chunks[3])
    save = pltpu.make_async_copy(g.at[x], state_out, out_sem.at[0])
    save.start()
    attend(chunks[3], last=True)
    for cp in started[sent:]:
        cp.wait_send()
    save.wait()


def last(read, state, high, low, state_out, pix_out, buffer, sem):
    copies = [pltpu.make_async_copy(state, state_out, sem.at[0])]
    copies[0].start()
    for k in range(2):
        rows = pl.ds(k * HALF, HALF)
        buffer[rows, :] = dot3(split(read[rows, :]), (high[...], low[...]), NN)
        cp = pltpu.make_async_copy(buffer.at[rows], pix_out.at[rows], sem.at[1 + k])
        cp.start()
        copies.append(cp)
    for cp in copies:
        cp.wait()


def shards(latents, pixel_keys, pixel_values, norm_gain, w_key, w_value, pixel_queries):
    operands = (latents, pixel_keys, pixel_values, norm_gain.reshape(1, D), w_key, w_value, pixel_queries)
    in_hbm = pl.BlockSpec(memory_space=pltpu.HBM)
    big = pltpu.VMEM((ROWS, D), F32)
    half = pltpu.VMEM((ROWS, D), BF16)
    dma = pltpu.SemaphoreType.DMA
    whole, rounded = jax.ShapeDtypeStruct((ROWS, D), F32), jax.ShapeDtypeStruct((D, D), BF16)
    in_vmem = pl.BlockSpec(memory_space=pltpu.VMEM)
    state, read, high, low = pl.pallas_call(
        kernel,
        out_shape=(whole, whole, rounded, rounded),
        in_specs=[in_hbm] * 7,
        out_specs=(in_vmem,) * 4,
        scratch_shapes=[
            big, big, big, pltpu.VMEM((1, D), F32), big, big, big,
            half, half, half, half, half, half,
            pltpu.VMEM((NY, SLAB, 128), F32),
            pltpu.VMEM((NY, SLAB, 128), F32),
            pltpu.VMEM((NY, SLAB, 128), F32),
            pltpu.VMEM((NY, SLAB, 128), F32),
            pltpu.VMEM((NY, SLAB, 128), F32),
            pltpu.VMEM((NZ, PIECE, 128), F32),
            pltpu.VMEM((NZ, PIECE, 128), F32),
            pltpu.VMEM((NX, ROWS, D), F32),
            big,
            pltpu.VMEM((ROWS, 128), F32),
            pltpu.VMEM((ROWS, 128), F32),
            dma((7,)), dma((1,)),
            dma((NY,)), dma((NY,)), dma((NY,)), dma((NY,)),
            dma((NZ,)), dma((NZ,)), dma((NZ,)), dma((NZ,)),
            dma((2, NY)), dma((2, NY)), dma((12,)), dma((12,)),
            dma((14,)), dma((14,)),
        ],
        compiler_params=pltpu.CompilerParams(
            collective_id=0, has_side_effects=True, vmem_limit_bytes=50 << 20
        ),
        name="perceiver",
    )(*(pltpu.with_memory_space_constraint(v, pltpu.HBM) for v in operands))
    return pl.pallas_call(
        last,
        out_shape=(whole, whole),
        in_specs=[in_vmem] * 4,
        out_specs=(in_hbm, in_hbm),
        scratch_shapes=[big, dma((3,))],
        compiler_params=pltpu.CompilerParams(vmem_limit_bytes=16 << 20),
        name="values",
    )(read, state, high, low)


def solution(mesh):
    in_specs = (P("lat", None), P("pix", None), P("pix", None), P(), P(), P(), P("pix", None))
    out_specs = (P("lat", None), P("pix", None))
    return jax.shard_map(shards, mesh=mesh, in_specs=in_specs, out_specs=out_specs, check_vma=False)
```

```python
import functools

import jax
import jax.numpy as jnp
from jax import lax
from jax.experimental import pallas as pl
from jax.experimental.pallas import tpu as pltpu
from jax.sharding import PartitionSpec as P

MESH = pl.DeviceIdType.MESH
F32, BF16 = jnp.float32, jnp.bfloat16
D = 512
NY, NZ, NX = 4, 8, 4
ROWS = 512
HALF = ROWS // 2
GROUP = 8
TILES = D // 128
PIECE = TILES * GROUP + 1
PART = TILES * NZ // 2 * GROUP
TOPS, TOTALS = slice(PART, PART + 8), slice(PART + 8, PART + 16)
SLAB = 2 * PART + 16
NN = (((1,), (0,)), ((), ()))
NT = (((1,), (1,)), ((), ()))
SCALE = 512.0**-0.5
BAND = 256


def tile_of(t, zz):
    r = (zz // 4) * (PART + 16) + (t * 4 + zz % 4) * GROUP
    return slice(r, r + GROUP)


def split(value):
    high = value.astype(BF16)
    return high, (value - high.astype(F32)).astype(BF16)


def dot3(a, b, dims):
    def one(u, v):
        return lax.dot_general(u, v, dims, preferred_element_type=F32)

    return one(a[0], b[0]) + (one(a[0], b[1]) + one(a[1], b[0]))


def kernel(
    lat_in, keys_in, vals_in, gain_in, wk_in, wv_in, q_in, state_out, read_out, wvh, wvl,
    lat, keys, vals, gain, wk, wv, q,
    kh, kl, vh, vl, qh, ql,
    slab_send, slab_own, slab_sib, slab_far, slab_r, piece, piece_r,
    g, acc, mx, tot,
    in_sem, out_sem, a0s, a0r, a1s, a1r, a2s, a2r, g1s, g1r, g2s, g2r, g3s, g3r, cs, cr,
):
    p = lax.axis_index("pix")
    x = lax.axis_index("lat")
    c = lax.rem(p, 2)
    y = lax.rem(p // 2, NY)
    z = p // (2 * NY)

    def at(zz, yy, cc, xx):
        return ((zz * NY + yy) * 2 + cc, xx)

    sib = at(z, y, 1 - c, x)

    def ypeer(d):
        return at(z, lax.rem(y + d + NY, NY), c, x)

    def zpeer(d):
        return at(lax.rem(z + d + NZ, NZ), y, c, x)

    def xpeer(d):
        return at(z, y, c, lax.rem(x + d + NX, NX))

    loads = []
    for k, (src, dst) in enumerate(
        [(lat_in, lat), (keys_in, keys), (vals_in, vals), (q_in, q), (wk_in, wk), (gain_in, gain), (wv_in, wv)]
    ):
        loads.append(pltpu.make_async_copy(src, dst, in_sem.at[k]))
    for cp in loads[:3]:
        cp.start()

    barrier = pltpu.get_barrier_semaphore()
    peers = (
        [sib]
        + [ypeer(d) for d in range(1, NY)]
        + [zpeer(d) for d in range(1, NZ)]
        + [xpeer(d) for d in range(1, NX)]
    )
    for dev in peers:
        pl.semaphore_signal(barrier, inc=1, device_id=dev, device_id_type=MESH)

    def remote(src, dst, ss, rs, dev):
        return pltpu.make_async_remote_copy(
            src_ref=src, dst_ref=dst, send_sem=ss, recv_sem=rs, device_id=dev, device_id_type=MESH
        )

    started = []

    def send(*args, keep=True):
        cp = remote(*args)
        cp.start()
        if keep:
            started.append(cp)
        return cp

    lanes = lax.broadcasted_iota(jnp.int32, (GROUP, 128), 1)
    sublanes = lax.broadcasted_iota(jnp.int32, (GROUP, 128), 0)

    loads[0].wait()
    loads[1].wait()
    kh[...], kl[...] = split(keys[...])

    def first_scores(which):
        lh = split(lat[pl.ds(pl.multiple_of(which * HALF, HALF), HALF), :])
        return dot3(lh, (kh[...], kl[...]), NT) * SCALE

    def first_read(s, slab):
        top = jnp.max(s, axis=1, keepdims=True)
        w = jnp.exp(s - top)
        total = jnp.sum(w, axis=1, keepdims=True)
        o = dot3(split(w), (vh[...], vl[...]), NN)
        for yy in range(NY):
            tops = jnp.zeros((GROUP, 128), F32)
            totals = jnp.zeros((GROUP, 128), F32)
            for zz in range(NZ):
                r = (zz // 4) * 128 + yy * 32 + (zz % 4) * GROUP
                tops = jnp.where(lanes == zz, top[r : r + GROUP], tops)
                totals = jnp.where(lanes == zz, total[r : r + GROUP], totals)
                for t in range(TILES):
                    slab[yy, tile_of(t, zz), :] = o[r : r + GROUP, t * 128 : (t + 1) * 128]
            slab[yy, TOPS, :] = tops
            slab[yy, TOTALS, :] = totals

    away = first_scores(1 - c)
    loads[2].wait()
    for cp in loads[3:]:
        cp.start()
    vh[...], vl[...] = split(vals[...])
    here = first_scores(c)
    first_read(away, slab_send)
    pl.semaphore_wait(barrier, len(peers))
    order = (2, 1, 3, 0)
    siblings = {}
    for d in order:
        yy = lax.rem(y + d, NY)
        siblings[d] = send(slab_send.at[yy], slab_sib.at[yy], a0s.at[d], a0r.at[d], sib)
    first_read(here, slab_own)

    def merge(into, d, tops, totals, others, zs, mask=None):
        old, new = into[d, TOPS, :], tops
        if mask is not None:
            new = jnp.where(mask, new, old)
        m = jnp.maximum(old, new)
        a, b = jnp.exp(old - m), jnp.exp(new - m)
        added = b * totals
        if mask is not None:
            added = jnp.where(mask, added, 0.0)
        into[d, TOPS, :] = m
        into[d, TOTALS, :] = a * into[d, TOTALS, :] + added
        for zz in zs:
            az, bz = a[:, zz : zz + 1], b[:, zz : zz + 1]
            for t in range(TILES):
                r = tile_of(t, zz)
                into[d, r, :] = az * into[d, r, :] + bz * others(r)

    def own_slab(d):
        yy = lax.rem(y + d, NY)
        siblings[d].wait_recv()
        merge(
            slab_own, yy, slab_sib[yy, TOPS, :], slab_sib[yy, TOTALS, :], lambda r: slab_sib[yy, r, :], range(NZ)
        )
        return yy

    front, back = pl.ds(0, PART + 16), pl.ds(PART, PART + 16)
    front_only, back_only = pl.ds(0, PART), pl.ds(PART + 16, PART)
    two_on = own_slab(2)
    through = (
        send(slab_own.at[two_on, front], slab_far.at[0, front], a1s.at[0], a1r.at[0], ypeer(1)),
        send(slab_own.at[two_on, back], slab_far.at[1, back], a1s.at[1], a1r.at[1], ypeer(3)),
    )
    to_y = []
    after = own_slab(1)
    to_y.append(send(slab_own.at[after, back_only], slab_r.at[1, back_only], a1s.at[2], a1r.at[2], ypeer(1)))
    before = own_slab(3)
    to_y.append(send(slab_own.at[before, front_only], slab_r.at[3, front_only], a1s.at[3], a1r.at[3], ypeer(3)))
    for k, (yy, zs, mask, rows, slot, d) in enumerate(
        ((after, range(4), lanes < 4, front, 1, 1), (before, range(4, NZ), lanes >= 4, back, 3, 3))
    ):
        through[k].wait_recv()
        merge(
            slab_own, yy, slab_far[k, TOPS, :], slab_far[k, TOTALS, :], lambda r, k=k: slab_far[k, r, :], zs, mask
        )
        to_y.append(send(slab_own.at[yy, rows], slab_r.at[slot, rows], a1s.at[4 + k], a1r.at[4 + k], ypeer(d)))
    own_slab(0)

    for k in (3, 4, 5):
        loads[k].wait()
    scaled = dot3(split(q[...]), split(wk[...]), NT) * (gain[...] * SCALE)
    qh[...], ql[...] = split(scaled)

    for cp in to_y:
        cp.wait_recv()
    parts = [slab_own.at[y], slab_r.at[1], slab_r.at[3]]
    tops = [s[TOPS, :] for s in parts]
    m = functools.reduce(jnp.maximum, tops)
    scales = [jnp.exp(v - m) for v in tops]
    total = functools.reduce(jnp.add, [s * v[TOTALS, :] for s, v in zip(scales, parts)])
    for zz in range(NZ):
        cols = [s[:, zz : zz + 1] for s in scales]
        for t in range(TILES):
            r = tile_of(t, zz)
            piece[zz, t * GROUP : (t + 1) * GROUP, :] = functools.reduce(
                jnp.add, [u * v[r, :] for u, v in zip(cols, parts)]
            )
        both = jnp.where(lanes < GROUP, m[:, zz : zz + 1], total[:, zz : zz + 1])
        piece[zz, TILES * GROUP : PIECE, :] = jnp.sum(
            jnp.where(lax.rem(lanes, GROUP) == sublanes, both, 0.0), axis=0, keepdims=True
        )

    z_order = (4, 3, 5, 2, 6, 1, 7)
    to_z = {}
    for d in z_order:
        zz = lax.rem(z + d, NZ)
        to_z[d] = send(piece.at[zz], piece_r.at[d], a2s.at[d], a2r.at[d], zpeer(d))
    loads[6].wait()
    wvh[...], wvl[...] = split(wv[...])
    for d in z_order:
        to_z[d].wait_recv()
    parts = [piece.at[z]] + [piece_r.at[d] for d in range(1, NZ)]
    stats = [jnp.broadcast_to(v[TILES * GROUP : PIECE, :], (GROUP, 128)) for v in parts]
    tops = [jnp.sum(jnp.where(lanes == sublanes, v, 0.0), axis=1, keepdims=True) for v in stats]
    totals = [jnp.sum(jnp.where(lanes == sublanes + GROUP, v, 0.0), axis=1, keepdims=True) for v in stats]
    m = functools.reduce(jnp.maximum, tops)
    scales = [jnp.exp(v - m) for v in tops]
    total = functools.reduce(jnp.add, [s * v for s, v in zip(scales, totals)])
    row = pl.multiple_of(c * HALF + (z // 4) * 128 + y * 32 + lax.rem(z, 4) * GROUP, GROUP)
    for t in range(TILES):
        o = functools.reduce(
            jnp.add, [s * v[t * GROUP : (t + 1) * GROUP, :] for s, v in zip(scales, parts)]
        )
        cols = slice(t * 128, (t + 1) * 128)
        g[x, pl.ds(row, GROUP), cols] = lat[pl.ds(row, GROUP), cols] + o / total

    mine = g.at[x, pl.ds(row, GROUP)]
    gather_z = {d: send(mine, mine, g1s.at[d], g1r.at[d], zpeer(d)) for d in z_order}
    for d in z_order:
        gather_z[d].wait_recv()
    low = g.at[x, pl.ds(pl.multiple_of(c * HALF + y * 32, 32), 32)]
    high = g.at[x, pl.ds(pl.multiple_of(c * HALF + 128 + y * 32, 32), 32)]
    near = (1, 3, 2)
    second = {}
    for d in near:
        second["y", d] = send(low, low, g2s.at[0, d], g2r.at[0, d], ypeer(d))
        second["x", d] = send(high, high, g2s.at[1, d], g2r.at[1, d], xpeer(d))

    def low_of(xx, cc, part):
        first, count = {"all": (0, 128), "A": (0, 64), "B": (64, 64)}[part]
        return g.at[xx, pl.ds(pl.multiple_of(cc * HALF + first, 64), count)]

    def high_of(yy, cc, part):
        blocks = {"all": pl.ds(0, 4), "A": pl.ds(0, 2), "B": pl.ds(2, 2)}[part]
        return g.at[blocks, pl.ds(pl.multiple_of(cc * HALF + 128 + yy * 32, 32), 32)]

    def source(axis, d, cc, part):
        if axis == "x":
            return low_of(lax.rem(x - d + NX, NX), cc, part)
        return high_of(lax.rem(y - d + NY, NY), cc, part)

    slots = {}
    for axis in "xy":
        for d, part in ((1, "A"), (3, "B"), (1, "B"), (3, "A"), (2, "A"), (2, "B")):
            slots[axis, d, part] = len(slots)
    third = {}

    def push(axis, back, d, part):
        step = (d - back) % 4
        k = slots[axis, d, part]
        ref = source(axis, back, c, part)
        third[axis, d, part] = send(
            ref, ref, g3s.at[k], g3r.at[k], xpeer(step) if axis == "x" else ypeer(step),
        )

    earlier = len(started)
    for axis, before in (("x", "y"), ("y", "x")):
        for d in near:
            second[before, d].wait_recv()
        for d, part in ((1, "A"), (3, "B"), (1, "B"), (3, "A")):
            push(axis, 0, d, part)

    def wide(value, times):
        return jnp.concatenate([value] * times, axis=1)

    def attend(chunk, cores, start=False, last=False):
        blocks = [source(axis, d, cc, part)[...] for axis, d, part in chunk for cc in cores]
        n = jnp.concatenate([b.reshape(-1, D) for b in blocks], axis=0)
        n = n * (1.0 / jnp.sqrt(jnp.mean(n * n, axis=1, keepdims=True) + 1e-6))
        nh = split(n)
        bands = [slice(r, r + BAND) for r in range(0, ROWS, BAND)]

        def scores(band):
            return dot3((qh[band, :], ql[band, :]), nh, NT)

        ahead = scores(bands[0])
        for k, band in enumerate(bands):
            s = ahead
            if k + 1 < len(bands):
                ahead = scores(bands[k + 1])
            columns = s.shape[1] // 128
            top = jnp.broadcast_to(jnp.max(s, axis=1, keepdims=True), (BAND, 128))
            m = top if start else jnp.maximum(mx[band, :], top)
            w = jnp.exp(s - wide(m, columns))
            total = functools.reduce(jnp.add, [w[:, t * 128 : (t + 1) * 128] for t in range(columns)])
            read = dot3(split(w), nh, NN)
            if not start:
                fade = jnp.exp(mx[band, :] - m)
                total = tot[band, :] * fade + total
                read = acc[band, :] * wide(fade, TILES) + read
            if last:
                read_out[band, :] = read / jnp.sum(total, axis=1, keepdims=True) * gain[...]
            else:
                mx[band, :] = m
                tot[band, :] = total
                acc[band, :] = read

    chunks = [
        [("x", 0, "all"), ("y", 0, "all")],
        [("x", 1, "A"), ("y", 1, "A"), ("x", 3, "B"), ("y", 3, "B")],
        [("x", 1, "B"), ("y", 1, "B"), ("x", 3, "A"), ("y", 3, "A")],
        [("x", 2, "A"), ("x", 2, "B"), ("y", 2, "A"), ("y", 2, "B")],
    ]
    passed = {}

    def pass_on(chunk):
        for axis, d, part in chunk:
            if d:
                third[axis, d, part].wait_recv()
            if (d, part) == (1, "A"):
                push(axis, 1, 2, "A")
            if (d, part) == (3, "B"):
                push(axis, 3, 2, "B")
            ref = source(axis, d, c, part)
            k = len(passed)
            passed[axis, d, part] = send(ref, ref, cs.at[k], cr.at[k], sib)

    def wait_for(chunk):
        for item in chunk:
            passed[item].wait_recv()

    near = chunks[1] + chunks[2]
    far = chunks[3]
    pass_on(chunks[0])
    wait_for(chunks[0])
    attend(chunks[0], (0, 1), start=True)
    for cp in started[:earlier]:
        cp.wait_send()
    pass_on(near)
    sent = len(started)
    attend(near, (c,))
    wait_for(near)
    attend(near, (1 - c,))
    pass_on(far)
    attend(far, (c,))
    for cp in started[earlier:sent]:
        cp.wait_send()
    wait_for(far)
    save = pltpu.make_async_copy(g.at[x], state_out, out_sem.at[0])
    save.start()
    attend(far, (1 - c,), last=True)
    for cp in started[sent:]:
        cp.wait_send()
    save.wait()


def last(read, state, high, low, state_out, pix_out, buffer, sem):
    copies = [pltpu.make_async_copy(state, state_out, sem.at[0])]
    copies[0].start()
    for k in range(2):
        rows = pl.ds(k * HALF, HALF)
        buffer[rows, :] = dot3(split(read[rows, :]), (high[...], low[...]), NN)
        cp = pltpu.make_async_copy(buffer.at[rows], pix_out.at[rows], sem.at[1 + k])
        cp.start()
        copies.append(cp)
    for cp in copies:
        cp.wait()


def shards(latents, pixel_keys, pixel_values, norm_gain, w_key, w_value, pixel_queries):
    operands = (latents, pixel_keys, pixel_values, norm_gain.reshape(1, D), w_key, w_value, pixel_queries)
    in_hbm = pl.BlockSpec(memory_space=pltpu.HBM)
    big = pltpu.VMEM((ROWS, D), F32)
    half = pltpu.VMEM((ROWS, D), BF16)
    dma = pltpu.SemaphoreType.DMA
    whole, rounded = jax.ShapeDtypeStruct((ROWS, D), F32), jax.ShapeDtypeStruct((D, D), BF16)
    in_vmem = pl.BlockSpec(memory_space=pltpu.VMEM)
    state, read, high, low = pl.pallas_call(
        kernel,
        out_shape=(whole, whole, rounded, rounded),
        in_specs=[in_hbm] * 7,
        out_specs=(in_vmem,) * 4,
        scratch_shapes=[
            big, big, big, pltpu.VMEM((1, D), F32), big, big, big,
            half, half, half, half, half, half,
            pltpu.VMEM((NY, SLAB, 128), F32),
            pltpu.VMEM((NY, SLAB, 128), F32),
            pltpu.VMEM((NY, SLAB, 128), F32),
            pltpu.VMEM((2, SLAB, 128), F32),
            pltpu.VMEM((NY, SLAB, 128), F32),
            pltpu.VMEM((NZ, PIECE, 128), F32),
            pltpu.VMEM((NZ, PIECE, 128), F32),
            pltpu.VMEM((NX, ROWS, D), F32),
            big,
            pltpu.VMEM((ROWS, 128), F32),
            pltpu.VMEM((ROWS, 128), F32),
            dma((7,)), dma((1,)),
            dma((NY,)), dma((NY,)), dma((6,)), dma((6,)),
            dma((NZ,)), dma((NZ,)), dma((NZ,)), dma((NZ,)),
            dma((2, NY)), dma((2, NY)), dma((12,)), dma((12,)),
            dma((14,)), dma((14,)),
        ],
        compiler_params=pltpu.CompilerParams(
            collective_id=0, has_side_effects=True, vmem_limit_bytes=50 << 20
        ),
        name="perceiver",
    )(*(pltpu.with_memory_space_constraint(v, pltpu.HBM) for v in operands))
    return pl.pallas_call(
        last,
        out_shape=(whole, whole),
        in_specs=[in_vmem] * 4,
        out_specs=(in_hbm, in_hbm),
        scratch_shapes=[big, dma((3,))],
        compiler_params=pltpu.CompilerParams(vmem_limit_bytes=16 << 20),
        name="values",
    )(read, state, high, low)


def solution(mesh):
    in_specs = (P("lat", None), P("pix", None), P("pix", None), P(), P(), P(), P("pix", None))
    out_specs = (P("lat", None), P("pix", None))
    return jax.shard_map(shards, mesh=mesh, in_specs=in_specs, out_specs=out_specs, check_vma=False)
```

```python
import functools

import jax
import jax.numpy as jnp
from jax import lax
from jax.experimental import pallas as pl
from jax.experimental.pallas import tpu as pltpu
from jax.sharding import PartitionSpec as P

MESH = pl.DeviceIdType.MESH
F32, BF16 = jnp.float32, jnp.bfloat16
D = 512
NY, NZ, NX = 4, 8, 4
ROWS = 512
HALF = ROWS // 2
GROUP = 8
TILES = D // 128
PIECE = TILES * GROUP + 1
PART = TILES * NZ // 2 * GROUP
TOPS, TOTALS = slice(PART, PART + 8), slice(PART + 8, PART + 16)
SLAB = 2 * PART + 16
NN = (((1,), (0,)), ((), ()))
NT = (((1,), (1,)), ((), ()))
SCALE = 512.0**-0.5
BAND = 256


def tile_of(t, zz):
    r = (zz // 4) * (PART + 16) + (t * 4 + zz % 4) * GROUP
    return slice(r, r + GROUP)


def split(value):
    high = value.astype(BF16)
    return high, (value - high.astype(F32)).astype(BF16)


def dot3(a, b, dims):
    def one(u, v):
        return lax.dot_general(u, v, dims, preferred_element_type=F32)

    return one(a[0], b[0]) + (one(a[0], b[1]) + one(a[1], b[0]))


def kernel(
    lat_in, keys_in, vals_in, gain_in, wk_in, wv_in, q_in, state_out, read_out, wvh, wvl,
    lat, keys, vals, gain, wk, wv, q,
    kh, kl, vh, vl, qh, ql,
    slab_send, slab_own, slab_sib, slab_far, slab_r, piece, piece_r,
    g, acc, mx, tot,
    in_sem, out_sem, a0s, a0r, a1s, a1r, a2s, a2r, g1s, g1r, g2s, g2r, g3s, g3r, cs, cr,
):
    p = lax.axis_index("pix")
    x = lax.axis_index("lat")
    c = lax.rem(p, 2)
    y = lax.rem(p // 2, NY)
    z = p // (2 * NY)

    def at(zz, yy, cc, xx):
        return ((zz * NY + yy) * 2 + cc, xx)

    sib = at(z, y, 1 - c, x)

    def ypeer(d):
        return at(z, lax.rem(y + d + NY, NY), c, x)

    def zpeer(d):
        return at(lax.rem(z + d + NZ, NZ), y, c, x)

    def xpeer(d):
        return at(z, y, c, lax.rem(x + d + NX, NX))

    loads = []
    for k, (src, dst) in enumerate(
        [(lat_in, lat), (keys_in, keys), (vals_in, vals), (q_in, q), (wk_in, wk), (gain_in, gain), (wv_in, wv)]
    ):
        loads.append(pltpu.make_async_copy(src, dst, in_sem.at[k]))
    for cp in loads[:3]:
        cp.start()

    barrier = pltpu.get_barrier_semaphore()
    peers = (
        [sib]
        + [ypeer(d) for d in range(1, NY)]
        + [zpeer(d) for d in range(1, NZ)]
        + [xpeer(d) for d in range(1, NX)]
    )
    for dev in peers:
        pl.semaphore_signal(barrier, inc=1, device_id=dev, device_id_type=MESH)

    def remote(src, dst, ss, rs, dev):
        return pltpu.make_async_remote_copy(
            src_ref=src, dst_ref=dst, send_sem=ss, recv_sem=rs, device_id=dev, device_id_type=MESH
        )

    started = []

    def send(*args, keep=True):
        cp = remote(*args)
        cp.start()
        if keep:
            started.append(cp)
        return cp

    lanes = lax.broadcasted_iota(jnp.int32, (GROUP, 128), 1)
    sublanes = lax.broadcasted_iota(jnp.int32, (GROUP, 128), 0)

    loads[0].wait()
    loads[1].wait()
    kh[...], kl[...] = split(keys[...])

    def first_scores(which):
        lh = split(lat[pl.ds(pl.multiple_of(which * HALF, HALF), HALF), :])
        return dot3(lh, (kh[...], kl[...]), NT) * SCALE

    def first_read(s, slab):
        top = jnp.max(s, axis=1, keepdims=True)
        w = jnp.exp(s - top)
        total = jnp.sum(w, axis=1, keepdims=True)
        o = dot3(split(w), (vh[...], vl[...]), NN)
        for yy in range(NY):
            tops = jnp.zeros((GROUP, 128), F32)
            totals = jnp.zeros((GROUP, 128), F32)
            for zz in range(NZ):
                r = (zz // 4) * 128 + yy * 32 + (zz % 4) * GROUP
                tops = jnp.where(lanes == zz, top[r : r + GROUP], tops)
                totals = jnp.where(lanes == zz, total[r : r + GROUP], totals)
                for t in range(TILES):
                    slab[yy, tile_of(t, zz), :] = o[r : r + GROUP, t * 128 : (t + 1) * 128]
            slab[yy, TOPS, :] = tops
            slab[yy, TOTALS, :] = totals

    away = first_scores(1 - c)
    loads[2].wait()
    for cp in loads[3:]:
        cp.start()
    vh[...], vl[...] = split(vals[...])
    here = first_scores(c)
    first_read(away, slab_send)
    pl.semaphore_wait(barrier, len(peers))
    order = (2, 1, 3, 0)
    siblings = {}
    for d in order:
        yy = lax.rem(y + d, NY)
        siblings[d] = send(slab_send.at[yy], slab_sib.at[yy], a0s.at[d], a0r.at[d], sib)
    first_read(here, slab_own)

    def merge(into, d, tops, totals, others, zs, mask=None):
        old, new = into[d, TOPS, :], tops
        if mask is not None:
            new = jnp.where(mask, new, old)
        m = jnp.maximum(old, new)
        a, b = jnp.exp(old - m), jnp.exp(new - m)
        added = b * totals
        if mask is not None:
            added = jnp.where(mask, added, 0.0)
        into[d, TOPS, :] = m
        into[d, TOTALS, :] = a * into[d, TOTALS, :] + added
        for zz in zs:
            az, bz = a[:, zz : zz + 1], b[:, zz : zz + 1]
            for t in range(TILES):
                r = tile_of(t, zz)
                into[d, r, :] = az * into[d, r, :] + bz * others(r)

    def own_slab(d):
        yy = lax.rem(y + d, NY)
        siblings[d].wait_recv()
        merge(
            slab_own, yy, slab_sib[yy, TOPS, :], slab_sib[yy, TOTALS, :], lambda r: slab_sib[yy, r, :], range(NZ)
        )
        return yy

    front, back = pl.ds(0, PART + 16), pl.ds(PART, PART + 16)
    front_only, back_only = pl.ds(0, PART), pl.ds(PART + 16, PART)
    two_on = own_slab(2)
    through = (
        send(slab_own.at[two_on, front], slab_far.at[0, front], a1s.at[0], a1r.at[0], ypeer(1)),
        send(slab_own.at[two_on, back], slab_far.at[1, back], a1s.at[1], a1r.at[1], ypeer(3)),
    )
    to_y = []
    after = own_slab(1)
    to_y.append(send(slab_own.at[after, back_only], slab_r.at[1, back_only], a1s.at[2], a1r.at[2], ypeer(1)))
    before = own_slab(3)
    to_y.append(send(slab_own.at[before, front_only], slab_r.at[3, front_only], a1s.at[3], a1r.at[3], ypeer(3)))
    for k, (yy, zs, mask, rows, slot, d) in enumerate(
        ((after, range(4), lanes < 4, front, 1, 1), (before, range(4, NZ), lanes >= 4, back, 3, 3))
    ):
        through[k].wait_recv()
        merge(
            slab_own, yy, slab_far[k, TOPS, :], slab_far[k, TOTALS, :], lambda r, k=k: slab_far[k, r, :], zs, mask
        )
        to_y.append(send(slab_own.at[yy, rows], slab_r.at[slot, rows], a1s.at[4 + k], a1r.at[4 + k], ypeer(d)))
    own_slab(0)

    for k in (3, 4, 5):
        loads[k].wait()
    scaled = dot3(split(q[...]), split(wk[...]), NT) * (gain[...] * SCALE)
    qh[...], ql[...] = split(scaled)

    for cp in to_y:
        cp.wait_recv()
    parts = [slab_own.at[y], slab_r.at[1], slab_r.at[3]]
    tops = [s[TOPS, :] for s in parts]
    m = functools.reduce(jnp.maximum, tops)
    scales = [jnp.exp(v - m) for v in tops]
    total = functools.reduce(jnp.add, [s * v[TOTALS, :] for s, v in zip(scales, parts)])
    for zz in range(NZ):
        cols = [s[:, zz : zz + 1] for s in scales]
        for t in range(TILES):
            r = tile_of(t, zz)
            piece[zz, t * GROUP : (t + 1) * GROUP, :] = functools.reduce(
                jnp.add, [u * v[r, :] for u, v in zip(cols, parts)]
            )
        both = jnp.where(lanes < GROUP, m[:, zz : zz + 1], total[:, zz : zz + 1])
        piece[zz, TILES * GROUP : PIECE, :] = jnp.sum(
            jnp.where(lax.rem(lanes, GROUP) == sublanes, both, 0.0), axis=0, keepdims=True
        )

    z_order = (4, 3, 5, 2, 6, 1, 7)
    to_z = {}
    for d in z_order:
        zz = lax.rem(z + d, NZ)
        to_z[d] = send(piece.at[zz], piece_r.at[d], a2s.at[d], a2r.at[d], zpeer(d))
    loads[6].wait()
    wvh[...], wvl[...] = split(wv[...])
    for d in z_order:
        to_z[d].wait_recv()
    parts = [piece.at[z]] + [piece_r.at[d] for d in range(1, NZ)]
    stats = [jnp.broadcast_to(v[TILES * GROUP : PIECE, :], (GROUP, 128)) for v in parts]
    tops = [jnp.sum(jnp.where(lanes == sublanes, v, 0.0), axis=1, keepdims=True) for v in stats]
    totals = [jnp.sum(jnp.where(lanes == sublanes + GROUP, v, 0.0), axis=1, keepdims=True) for v in stats]
    m = functools.reduce(jnp.maximum, tops)
    scales = [jnp.exp(v - m) for v in tops]
    total = functools.reduce(jnp.add, [s * v for s, v in zip(scales, totals)])
    row = pl.multiple_of(c * HALF + (z // 4) * 128 + y * 32 + lax.rem(z, 4) * GROUP, GROUP)
    for t in range(TILES):
        o = functools.reduce(
            jnp.add, [s * v[t * GROUP : (t + 1) * GROUP, :] for s, v in zip(scales, parts)]
        )
        cols = slice(t * 128, (t + 1) * 128)
        g[x, pl.ds(row, GROUP), cols] = lat[pl.ds(row, GROUP), cols] + o / total

    mine = g.at[x, pl.ds(row, GROUP)]
    gather_z = {d: send(mine, mine, g1s.at[d], g1r.at[d], zpeer(d)) for d in z_order}
    for d in z_order:
        gather_z[d].wait_recv()
    low = g.at[x, pl.ds(pl.multiple_of(c * HALF + y * 32, 32), 32)]
    high = g.at[x, pl.ds(pl.multiple_of(c * HALF + 128 + y * 32, 32), 32)]
    near = (2, 1, 3)
    second = {}
    for d in near:
        second["y", d] = send(low, low, g2s.at[0, d], g2r.at[0, d], ypeer(d))
        second["x", d] = send(high, high, g2s.at[1, d], g2r.at[1, d], xpeer(d))

    def low_of(xx, cc, part):
        first, count = {"all": (0, 128), "A": (0, 64), "B": (64, 64)}[part]
        return g.at[xx, pl.ds(pl.multiple_of(cc * HALF + first, 64), count)]

    def high_of(yy, cc, part):
        blocks = {"all": pl.ds(0, 4), "A": pl.ds(0, 2), "B": pl.ds(2, 2)}[part]
        return g.at[blocks, pl.ds(pl.multiple_of(cc * HALF + 128 + yy * 32, 32), 32)]

    def source(axis, d, cc, part):
        if axis == "x":
            return low_of(lax.rem(x - d + NX, NX), cc, part)
        return high_of(lax.rem(y - d + NY, NY), cc, part)

    slots = {}
    for axis in "xy":
        for d, part in ((1, "A"), (3, "B"), (1, "B"), (3, "A"), (2, "A"), (2, "B")):
            slots[axis, d, part] = len(slots)
    third = {}

    def push(axis, back, d, part):
        step = (d - back) % 4
        k = slots[axis, d, part]
        ref = source(axis, back, c, part)
        third[axis, d, part] = send(
            ref, ref, g3s.at[k], g3r.at[k], xpeer(step) if axis == "x" else ypeer(step),
        )

    earlier = len(started)
    for axis, before in (("x", "y"), ("y", "x")):
        for d in near:
            second[before, d].wait_recv()
        for d, part in ((1, "A"), (3, "B"), (1, "B"), (3, "A")):
            push(axis, 0, d, part)

    def wide(value, times):
        return jnp.concatenate([value] * times, axis=1)

    def attend(chunk, cores, start=False, last=False):
        blocks = [source(axis, d, cc, part)[...] for axis, d, part in chunk for cc in cores]
        n = jnp.concatenate([b.reshape(-1, D) for b in blocks], axis=0)
        n = n * (1.0 / jnp.sqrt(jnp.mean(n * n, axis=1, keepdims=True) + 1e-6))
        nh = split(n)
        bands = [slice(r, r + BAND) for r in range(0, ROWS, BAND)]

        def scores(band):
            return dot3((qh[band, :], ql[band, :]), nh, NT)

        ahead = scores(bands[0])
        for k, band in enumerate(bands):
            s = ahead
            if k + 1 < len(bands):
                ahead = scores(bands[k + 1])
            columns = s.shape[1] // 128
            top = jnp.broadcast_to(jnp.max(s, axis=1, keepdims=True), (BAND, 128))
            m = top if start else jnp.maximum(mx[band, :], top)
            w = jnp.exp(s - wide(m, columns))
            total = functools.reduce(jnp.add, [w[:, t * 128 : (t + 1) * 128] for t in range(columns)])
            read = dot3(split(w), nh, NN)
            if not start:
                fade = jnp.exp(mx[band, :] - m)
                total = tot[band, :] * fade + total
                read = acc[band, :] * wide(fade, TILES) + read
            if last:
                read_out[band, :] = read / jnp.sum(total, axis=1, keepdims=True) * gain[...]
            else:
                mx[band, :] = m
                tot[band, :] = total
                acc[band, :] = read

    chunks = [
        [("x", 0, "all"), ("y", 0, "all")],
        [("x", 1, "A"), ("y", 1, "A"), ("x", 3, "B"), ("y", 3, "B")],
        [("x", 1, "B"), ("y", 1, "B"), ("x", 3, "A"), ("y", 3, "A")],
        [("x", 2, "A"), ("x", 2, "B"), ("y", 2, "A"), ("y", 2, "B")],
    ]
    passed = {}

    def pass_on(chunk):
        for axis, d, part in chunk:
            if d:
                third[axis, d, part].wait_recv()
            if (d, part) == (1, "A"):
                push(axis, 1, 2, "A")
            if (d, part) == (3, "B"):
                push(axis, 3, 2, "B")
            ref = source(axis, d, c, part)
            k = len(passed)
            passed[axis, d, part] = send(ref, ref, cs.at[k], cr.at[k], sib)

    def wait_for(chunk):
        for item in chunk:
            passed[item].wait_recv()

    near = chunks[1] + chunks[2]
    far = chunks[3]
    pass_on(chunks[0])
    for cp in started[:earlier]:
        cp.wait_send()
    wait_for(chunks[0])
    attend(chunks[0], (0, 1), start=True)
    pass_on(near)
    sent = len(started)
    attend(near, (c,))
    wait_for(near)
    attend(near, (1 - c,))
    pass_on(far)
    attend(far, (c,))
    for cp in started[earlier:sent]:
        cp.wait_send()
    wait_for(far)
    save = pltpu.make_async_copy(g.at[x], state_out, out_sem.at[0])
    save.start()
    attend(far, (1 - c,), last=True)
    for cp in started[sent:]:
        cp.wait_send()
    save.wait()


def last(read, state, high, low, state_out, pix_out, buffer, sem):
    copies = [pltpu.make_async_copy(state, state_out, sem.at[0])]
    copies[0].start()
    for k in range(2):
        rows = pl.ds(k * HALF, HALF)
        buffer[rows, :] = dot3(split(read[rows, :]), (high[...], low[...]), NN)
        cp = pltpu.make_async_copy(buffer.at[rows], pix_out.at[rows], sem.at[1 + k])
        cp.start()
        copies.append(cp)
    for cp in copies:
        cp.wait()


def shards(latents, pixel_keys, pixel_values, norm_gain, w_key, w_value, pixel_queries):
    operands = (latents, pixel_keys, pixel_values, norm_gain.reshape(1, D), w_key, w_value, pixel_queries)
    in_hbm = pl.BlockSpec(memory_space=pltpu.HBM)
    big = pltpu.VMEM((ROWS, D), F32)
    half = pltpu.VMEM((ROWS, D), BF16)
    dma = pltpu.SemaphoreType.DMA
    whole, rounded = jax.ShapeDtypeStruct((ROWS, D), F32), jax.ShapeDtypeStruct((D, D), BF16)
    in_vmem = pl.BlockSpec(memory_space=pltpu.VMEM)
    state, read, high, low = pl.pallas_call(
        kernel,
        out_shape=(whole, whole, rounded, rounded),
        in_specs=[in_hbm] * 7,
        out_specs=(in_vmem,) * 4,
        scratch_shapes=[
            big, big, big, pltpu.VMEM((1, D), F32), big, big, big,
            half, half, half, half, half, half,
            pltpu.VMEM((NY, SLAB, 128), F32),
            pltpu.VMEM((NY, SLAB, 128), F32),
            pltpu.VMEM((NY, SLAB, 128), F32),
            pltpu.VMEM((2, SLAB, 128), F32),
            pltpu.VMEM((NY, SLAB, 128), F32),
            pltpu.VMEM((NZ, PIECE, 128), F32),
            pltpu.VMEM((NZ, PIECE, 128), F32),
            pltpu.VMEM((NX, ROWS, D), F32),
            big,
            pltpu.VMEM((ROWS, 128), F32),
            pltpu.VMEM((ROWS, 128), F32),
            dma((7,)), dma((1,)),
            dma((NY,)), dma((NY,)), dma((6,)), dma((6,)),
            dma((NZ,)), dma((NZ,)), dma((NZ,)), dma((NZ,)),
            dma((2, NY)), dma((2, NY)), dma((12,)), dma((12,)),
            dma((14,)), dma((14,)),
        ],
        compiler_params=pltpu.CompilerParams(
            collective_id=0, has_side_effects=True, vmem_limit_bytes=50 << 20
        ),
        name="perceiver",
    )(*(pltpu.with_memory_space_constraint(v, pltpu.HBM) for v in operands))
    return pl.pallas_call(
        last,
        out_shape=(whole, whole),
        in_specs=[in_vmem] * 4,
        out_specs=(in_hbm, in_hbm),
        scratch_shapes=[big, dma((3,))],
        compiler_params=pltpu.CompilerParams(vmem_limit_bytes=16 << 20),
        name="values",
    )(read, state, high, low)


def solution(mesh):
    in_specs = (P("lat", None), P("pix", None), P("pix", None), P(), P(), P(), P("pix", None))
    out_specs = (P("lat", None), P("pix", None))
    return jax.shard_map(shards, mesh=mesh, in_specs=in_specs, out_specs=out_specs, check_vma=False)
```

```python
import functools

import jax
import jax.numpy as jnp
from jax import lax
from jax.experimental import pallas as pl
from jax.experimental.pallas import tpu as pltpu
from jax.sharding import PartitionSpec as P

MESH = pl.DeviceIdType.MESH
F32, BF16 = jnp.float32, jnp.bfloat16
D = 512
NY, NZ, NX = 4, 8, 4
ROWS = 512
HALF = ROWS // 2
GROUP = 8
TILES = D // 128
PIECE = TILES * GROUP + 1
PART = TILES * NZ // 2 * GROUP
TOPS, TOTALS = slice(PART, PART + 8), slice(PART + 8, PART + 16)
SLAB = 2 * PART + 16
NN = (((1,), (0,)), ((), ()))
NT = (((1,), (1,)), ((), ()))
SCALE = 512.0**-0.5
BAND = 256


def tile_of(t, zz):
    r = (zz // 4) * (PART + 16) + (t * 4 + zz % 4) * GROUP
    return slice(r, r + GROUP)


def split(value):
    high = value.astype(BF16)
    return high, (value - high.astype(F32)).astype(BF16)


def dot3(a, b, dims):
    def one(u, v):
        return lax.dot_general(u, v, dims, preferred_element_type=F32)

    return one(a[0], b[0]) + (one(a[0], b[1]) + one(a[1], b[0]))


def kernel(
    lat_in, keys_in, vals_in, gain_in, wk_in, wv_in, q_in, state_out, read_out, wvh, wvl,
    lat, keys, vals, gain, wk, wv, q,
    kh, kl, vh, vl, qh, ql,
    slab_send, slab_own, slab_sib, slab_far, slab_r, piece, piece_r,
    g, acc, mx, tot,
    in_sem, out_sem, a0s, a0r, a1s, a1r, a2s, a2r, g1s, g1r, g2s, g2r, g3s, g3r, cs, cr,
):
    p = lax.axis_index("pix")
    x = lax.axis_index("lat")
    c = lax.rem(p, 2)
    y = lax.rem(p // 2, NY)
    z = p // (2 * NY)

    def at(zz, yy, cc, xx):
        return ((zz * NY + yy) * 2 + cc, xx)

    sib = at(z, y, 1 - c, x)

    def ypeer(d):
        return at(z, lax.rem(y + d + NY, NY), c, x)

    def zpeer(d):
        return at(lax.rem(z + d + NZ, NZ), y, c, x)

    def xpeer(d):
        return at(z, y, c, lax.rem(x + d + NX, NX))

    loads = []
    for k, (src, dst) in enumerate(
        [(lat_in, lat), (keys_in, keys), (vals_in, vals), (q_in, q), (wk_in, wk), (gain_in, gain), (wv_in, wv)]
    ):
        loads.append(pltpu.make_async_copy(src, dst, in_sem.at[k]))
    for cp in loads[:3]:
        cp.start()

    barrier = pltpu.get_barrier_semaphore()
    peers = (
        [sib]
        + [ypeer(d) for d in range(1, NY)]
        + [zpeer(d) for d in range(1, NZ)]
        + [xpeer(d) for d in range(1, NX)]
    )
    for dev in peers:
        pl.semaphore_signal(barrier, inc=1, device_id=dev, device_id_type=MESH)

    def remote(src, dst, ss, rs, dev):
        return pltpu.make_async_remote_copy(
            src_ref=src, dst_ref=dst, send_sem=ss, recv_sem=rs, device_id=dev, device_id_type=MESH
        )

    started = []

    def send(*args, keep=True):
        cp = remote(*args)
        cp.start()
        if keep:
            started.append(cp)
        return cp

    lanes = lax.broadcasted_iota(jnp.int32, (GROUP, 128), 1)
    sublanes = lax.broadcasted_iota(jnp.int32, (GROUP, 128), 0)

    loads[0].wait()
    loads[1].wait()
    kh[...], kl[...] = split(keys[...])

    def first_scores(which):
        lh = split(lat[pl.ds(pl.multiple_of(which * HALF, HALF), HALF), :])
        return dot3(lh, (kh[...], kl[...]), NT) * SCALE

    def first_read(s, slab):
        top = jnp.max(s, axis=1, keepdims=True)
        w = jnp.exp(s - top)
        total = jnp.sum(w, axis=1, keepdims=True)
        o = dot3(split(w), (vh[...], vl[...]), NN)
        for yy in range(NY):
            tops = jnp.zeros((GROUP, 128), F32)
            totals = jnp.zeros((GROUP, 128), F32)
            for zz in range(NZ):
                r = (zz // 4) * 128 + yy * 32 + (zz % 4) * GROUP
                tops = jnp.where(lanes == zz, top[r : r + GROUP], tops)
                totals = jnp.where(lanes == zz, total[r : r + GROUP], totals)
                for t in range(TILES):
                    slab[yy, tile_of(t, zz), :] = o[r : r + GROUP, t * 128 : (t + 1) * 128]
            slab[yy, TOPS, :] = tops
            slab[yy, TOTALS, :] = totals

    away = first_scores(1 - c)
    loads[2].wait()
    for cp in loads[3:]:
        cp.start()
    vh[...], vl[...] = split(vals[...])
    here = first_scores(c)
    first_read(away, slab_send)
    pl.semaphore_wait(barrier, len(peers))
    order = (2, 1, 3, 0)
    siblings = {}
    for d in order:
        yy = lax.rem(y + d, NY)
        siblings[d] = send(slab_send.at[yy], slab_sib.at[yy], a0s.at[d], a0r.at[d], sib)
    first_read(here, slab_own)

    def merge(into, d, tops, totals, others, zs, mask=None):
        old, new = into[d, TOPS, :], tops
        if mask is not None:
            new = jnp.where(mask, new, old)
        m = jnp.maximum(old, new)
        a, b = jnp.exp(old - m), jnp.exp(new - m)
        added = b * totals
        if mask is not None:
            added = jnp.where(mask, added, 0.0)
        into[d, TOPS, :] = m
        into[d, TOTALS, :] = a * into[d, TOTALS, :] + added
        for zz in zs:
            az, bz = a[:, zz : zz + 1], b[:, zz : zz + 1]
            for t in range(TILES):
                r = tile_of(t, zz)
                into[d, r, :] = az * into[d, r, :] + bz * others(r)

    def own_slab(d):
        yy = lax.rem(y + d, NY)
        siblings[d].wait_recv()
        merge(
            slab_own, yy, slab_sib[yy, TOPS, :], slab_sib[yy, TOTALS, :], lambda r: slab_sib[yy, r, :], range(NZ)
        )
        return yy

    front, back = pl.ds(0, PART + 16), pl.ds(PART, PART + 16)
    front_only, back_only = pl.ds(0, PART), pl.ds(PART + 16, PART)
    two_on = own_slab(2)
    through = (
        send(slab_own.at[two_on, front], slab_far.at[0, front], a1s.at[0], a1r.at[0], ypeer(1)),
        send(slab_own.at[two_on, back], slab_far.at[1, back], a1s.at[1], a1r.at[1], ypeer(3)),
    )
    to_y = []
    after = own_slab(1)
    to_y.append(send(slab_own.at[after, back_only], slab_r.at[1, back_only], a1s.at[2], a1r.at[2], ypeer(1)))
    before = own_slab(3)
    to_y.append(send(slab_own.at[before, front_only], slab_r.at[3, front_only], a1s.at[3], a1r.at[3], ypeer(3)))
    for k, (yy, zs, mask, rows, slot, d) in enumerate(
        ((after, range(4), lanes < 4, front, 1, 1), (before, range(4, NZ), lanes >= 4, back, 3, 3))
    ):
        through[k].wait_recv()
        merge(
            slab_own, yy, slab_far[k, TOPS, :], slab_far[k, TOTALS, :], lambda r, k=k: slab_far[k, r, :], zs, mask
        )
        to_y.append(send(slab_own.at[yy, rows], slab_r.at[slot, rows], a1s.at[4 + k], a1r.at[4 + k], ypeer(d)))
    own_slab(0)

    for k in (3, 4, 5):
        loads[k].wait()
    scaled = dot3(split(q[...]), split(wk[...]), NT) * (gain[...] * SCALE)
    qh[...], ql[...] = split(scaled)

    for cp in to_y:
        cp.wait_recv()
    parts = [slab_own.at[y], slab_r.at[1], slab_r.at[3]]
    tops = [s[TOPS, :] for s in parts]
    m = functools.reduce(jnp.maximum, tops)
    scales = [jnp.exp(v - m) for v in tops]
    total = functools.reduce(jnp.add, [s * v[TOTALS, :] for s, v in zip(scales, parts)])
    for zz in range(NZ):
        cols = [s[:, zz : zz + 1] for s in scales]
        for t in range(TILES):
            r = tile_of(t, zz)
            piece[zz, t * GROUP : (t + 1) * GROUP, :] = functools.reduce(
                jnp.add, [u * v[r, :] for u, v in zip(cols, parts)]
            )
        both = jnp.where(lanes < GROUP, m[:, zz : zz + 1], total[:, zz : zz + 1])
        piece[zz, TILES * GROUP : PIECE, :] = jnp.sum(
            jnp.where(lax.rem(lanes, GROUP) == sublanes, both, 0.0), axis=0, keepdims=True
        )

    z_order = (4, 3, 5, 2, 6, 1, 7)
    to_z = {}
    for d in z_order:
        zz = lax.rem(z + d, NZ)
        to_z[d] = send(piece.at[zz], piece_r.at[d], a2s.at[d], a2r.at[d], zpeer(d))
    loads[6].wait()
    wvh[...], wvl[...] = split(wv[...])
    for d in z_order:
        to_z[d].wait_recv()
    parts = [piece.at[z]] + [piece_r.at[d] for d in range(1, NZ)]
    stats = [jnp.broadcast_to(v[TILES * GROUP : PIECE, :], (GROUP, 128)) for v in parts]
    tops = [jnp.sum(jnp.where(lanes == sublanes, v, 0.0), axis=1, keepdims=True) for v in stats]
    totals = [jnp.sum(jnp.where(lanes == sublanes + GROUP, v, 0.0), axis=1, keepdims=True) for v in stats]
    m = functools.reduce(jnp.maximum, tops)
    scales = [jnp.exp(v - m) for v in tops]
    total = functools.reduce(jnp.add, [s * v for s, v in zip(scales, totals)])
    row = pl.multiple_of(c * HALF + (z // 4) * 128 + y * 32 + lax.rem(z, 4) * GROUP, GROUP)
    for t in range(TILES):
        o = functools.reduce(
            jnp.add, [s * v[t * GROUP : (t + 1) * GROUP, :] for s, v in zip(scales, parts)]
        )
        cols = slice(t * 128, (t + 1) * 128)
        g[x, pl.ds(row, GROUP), cols] = lat[pl.ds(row, GROUP), cols] + o / total

    mine = g.at[x, pl.ds(row, GROUP)]
    gather_z = {d: send(mine, mine, g1s.at[d], g1r.at[d], zpeer(d)) for d in z_order}
    for d in z_order:
        gather_z[d].wait_recv()
    low = g.at[x, pl.ds(pl.multiple_of(c * HALF + y * 32, 32), 32)]
    high = g.at[x, pl.ds(pl.multiple_of(c * HALF + 128 + y * 32, 32), 32)]
    near = (2, 1, 3)
    second = {}
    for d in near:
        second["y", d] = send(low, low, g2s.at[0, d], g2r.at[0, d], ypeer(d))
        second["x", d] = send(high, high, g2s.at[1, d], g2r.at[1, d], xpeer(d))

    def low_of(xx, cc, part):
        first, count = {"all": (0, 128), "A": (0, 64), "B": (64, 64)}[part]
        return g.at[xx, pl.ds(pl.multiple_of(cc * HALF + first, 64), count)]

    def high_of(yy, cc, part):
        blocks = {"all": pl.ds(0, 4), "A": pl.ds(0, 2), "B": pl.ds(2, 2)}[part]
        return g.at[blocks, pl.ds(pl.multiple_of(cc * HALF + 128 + yy * 32, 32), 32)]

    def source(axis, d, cc, part):
        if axis == "x":
            return low_of(lax.rem(x - d + NX, NX), cc, part)
        return high_of(lax.rem(y - d + NY, NY), cc, part)

    slots = {}
    for axis in "xy":
        for d, part in ((1, "A"), (3, "B"), (1, "B"), (3, "A"), (2, "A"), (2, "B")):
            slots[axis, d, part] = len(slots)
    third = {}

    def push(axis, back, d, part):
        step = (d - back) % 4
        k = slots[axis, d, part]
        ref = source(axis, back, c, part)
        third[axis, d, part] = send(
            ref, ref, g3s.at[k], g3r.at[k], xpeer(step) if axis == "x" else ypeer(step),
        )

    earlier = len(started)
    for axis, before in (("x", "y"), ("y", "x")):
        for d in near:
            second[before, d].wait_recv()
        for d, part in ((1, "A"), (3, "B"), (1, "B"), (3, "A")):
            push(axis, 0, d, part)

    def wide(value, times):
        return jnp.concatenate([value] * times, axis=1)

    def attend(chunk, cores, start=False, last=False):
        blocks = [source(axis, d, cc, part)[...] for axis, d, part in chunk for cc in cores]
        n = jnp.concatenate([b.reshape(-1, D) for b in blocks], axis=0)
        n = n * (1.0 / jnp.sqrt(jnp.mean(n * n, axis=1, keepdims=True) + 1e-6))
        nh = split(n)
        bands = [slice(r, r + BAND) for r in range(0, ROWS, BAND)]

        def scores(band):
            return dot3((qh[band, :], ql[band, :]), nh, NT)

        ahead = scores(bands[0])
        for k, band in enumerate(bands):
            s = ahead
            if k + 1 < len(bands):
                ahead = scores(bands[k + 1])
            columns = s.shape[1] // 128
            top = jnp.broadcast_to(jnp.max(s, axis=1, keepdims=True), (BAND, 128))
            m = top if start else jnp.maximum(mx[band, :], top)
            w = jnp.exp(s - wide(m, columns))
            total = functools.reduce(jnp.add, [w[:, t * 128 : (t + 1) * 128] for t in range(columns)])
            read = dot3(split(w), nh, NN)
            if not start:
                fade = jnp.exp(mx[band, :] - m)
                total = tot[band, :] * fade + total
                read = acc[band, :] * wide(fade, TILES) + read
            if last:
                read_out[band, :] = read / jnp.sum(total, axis=1, keepdims=True) * gain[...]
            else:
                mx[band, :] = m
                tot[band, :] = total
                acc[band, :] = read

    chunks = [
        [("x", 0, "all"), ("y", 0, "all")],
        [("x", 1, "A"), ("y", 1, "A"), ("x", 3, "B"), ("y", 3, "B")],
        [("x", 1, "B"), ("y", 1, "B"), ("x", 3, "A"), ("y", 3, "A")],
        [("x", 2, "A"), ("x", 2, "B"), ("y", 2, "A"), ("y", 2, "B")],
    ]
    passed = {}

    def pass_on(chunk):
        for axis, d, part in chunk:
            if d:
                third[axis, d, part].wait_recv()
            if (d, part) == (1, "A"):
                push(axis, 1, 2, "A")
            if (d, part) == (3, "B"):
                push(axis, 3, 2, "B")
            ref = source(axis, d, c, part)
            k = len(passed)
            passed[axis, d, part] = send(ref, ref, cs.at[k], cr.at[k], sib)

    def wait_for(chunk):
        for item in chunk:
            passed[item].wait_recv()

    near = chunks[1] + chunks[2]
    far = chunks[3]
    pass_on(chunks[0])
    for cp in started[:earlier]:
        cp.wait_send()
    wait_for(chunks[0])
    attend(chunks[0], (0, 1), start=True)
    pass_on(chunks[1])
    attend(chunks[1], (c,))
    pass_on(chunks[2])
    sent = len(started)
    attend(chunks[2], (c,))
    wait_for(near)
    attend(near, (1 - c,))
    for cp in started[earlier:sent]:
        cp.wait_send()
    pass_on(far)
    attend(far, (c,))
    wait_for(far)
    save = pltpu.make_async_copy(g.at[x], state_out, out_sem.at[0])
    save.start()
    attend(far, (1 - c,), last=True)
    for cp in started[sent:]:
        cp.wait_send()
    save.wait()


def last(read, state, high, low, state_out, pix_out, buffer, sem):
    copies = [pltpu.make_async_copy(state, state_out, sem.at[0])]
    copies[0].start()
    for k in range(2):
        rows = pl.ds(k * HALF, HALF)
        buffer[rows, :] = dot3(split(read[rows, :]), (high[...], low[...]), NN)
        cp = pltpu.make_async_copy(buffer.at[rows], pix_out.at[rows], sem.at[1 + k])
        cp.start()
        copies.append(cp)
    for cp in copies:
        cp.wait()


def shards(latents, pixel_keys, pixel_values, norm_gain, w_key, w_value, pixel_queries):
    operands = (latents, pixel_keys, pixel_values, norm_gain.reshape(1, D), w_key, w_value, pixel_queries)
    in_hbm = pl.BlockSpec(memory_space=pltpu.HBM)
    big = pltpu.VMEM((ROWS, D), F32)
    half = pltpu.VMEM((ROWS, D), BF16)
    dma = pltpu.SemaphoreType.DMA
    whole, rounded = jax.ShapeDtypeStruct((ROWS, D), F32), jax.ShapeDtypeStruct((D, D), BF16)
    in_vmem = pl.BlockSpec(memory_space=pltpu.VMEM)
    state, read, high, low = pl.pallas_call(
        kernel,
        out_shape=(whole, whole, rounded, rounded),
        in_specs=[in_hbm] * 7,
        out_specs=(in_vmem,) * 4,
        scratch_shapes=[
            big, big, big, pltpu.VMEM((1, D), F32), big, big, big,
            half, half, half, half, half, half,
            pltpu.VMEM((NY, SLAB, 128), F32),
            pltpu.VMEM((NY, SLAB, 128), F32),
            pltpu.VMEM((NY, SLAB, 128), F32),
            pltpu.VMEM((2, SLAB, 128), F32),
            pltpu.VMEM((NY, SLAB, 128), F32),
            pltpu.VMEM((NZ, PIECE, 128), F32),
            pltpu.VMEM((NZ, PIECE, 128), F32),
            pltpu.VMEM((NX, ROWS, D), F32),
            big,
            pltpu.VMEM((ROWS, 128), F32),
            pltpu.VMEM((ROWS, 128), F32),
            dma((7,)), dma((1,)),
            dma((NY,)), dma((NY,)), dma((6,)), dma((6,)),
            dma((NZ,)), dma((NZ,)), dma((NZ,)), dma((NZ,)),
            dma((2, NY)), dma((2, NY)), dma((12,)), dma((12,)),
            dma((14,)), dma((14,)),
        ],
        compiler_params=pltpu.CompilerParams(
            collective_id=0, has_side_effects=True, vmem_limit_bytes=50 << 20
        ),
        name="perceiver",
    )(*(pltpu.with_memory_space_constraint(v, pltpu.HBM) for v in operands))
    return pl.pallas_call(
        last,
        out_shape=(whole, whole),
        in_specs=[in_vmem] * 4,
        out_specs=(in_hbm, in_hbm),
        scratch_shapes=[big, dma((3,))],
        compiler_params=pltpu.CompilerParams(vmem_limit_bytes=16 << 20),
        name="values",
    )(read, state, high, low)


def solution(mesh):
    in_specs = (P("lat", None), P("pix", None), P("pix", None), P(), P(), P(), P("pix", None))
    out_specs = (P("lat", None), P("pix", None))
    return jax.shard_map(shards, mesh=mesh, in_specs=in_specs, out_specs=out_specs, check_vma=False)
```
